256 devices in a mesh: subj: 16 (over y, x), slab: 16 (over z, core).
Axes of the slice: x: 4, y: 4, z: 8, core: 2. Of those that a mesh axis runs over, the one named last changes fastest.
Arguments:
- template: float32 [8192, 128], P('slab'), may hold values from -6 to 6
- images: float32 [16, 8192, 128], P('subj', 'slab'), may hold values from -6 to 6
- velocity: float32 [16, 3, 8192, 128], P('subj', None, 'slab'), may hold values from -6 to 6
- stiffness: float32 [8192, 128], P('slab'), may hold values from 0.1 to 1
- send_rows: int32 [16, 16, 16, 32], P('subj', 'slab'), may hold values from 0 to 511, as said below
- ref_slot: int32 [16, 8192, 8], P('subj', 'slab'), may hold values from 0 to 511, as said below
- columns: int32 [16, 8192, 8, 128], P('subj', 'slab'), may hold values from 0 to 127, as said below
- weights: bfloat16 [16, 8192, 8, 128], P('subj', 'slab'), may hold values from 0 to 0.25
Outputs:
- template_out: float32 [8192, 128], P('slab')
- velocity_out: float32 [16, 3, 8192, 128], P('subj', None, 'slab')
The draws below stay inside these ranges and needn't reach their ends.
Inputs may be any that keep to these rules, and one draw needn't show every extreme that they name: `send_rows`: local rows of the owner slab. `ref_slot`: for each subject and each owner k and destination slab j, the referenced c lie below a count of that pair between 16 and 32; for each subject one destination slab has the count 32 from every owner. columns[s, g, b, x] differs from x by at most 2.
All inputs are finite; a program needn't handle non-finite values.
Results may differ from the reference program's by a relative error of at most 0.0003.
Values sent between devices are 32-bit elements; how exact they have to be, the bound alone decides.
A program may use at most 64 MiB of HBM per device.

```python
import math
import jax
import jax.numpy as jnp
from jax import lax

W = 128
YR = 256
PLANES = 2
NB = 8
SMOOTH = 2
SLABS = 16
SUBJECTS = 16
ROWS = 512
NR = 8192
CAP = 32


def pair_counts(key):
    base_key = jax.random.fold_in(key, 11)
    count_key, full_key = jax.random.split(base_key)
    counts = jax.random.randint(count_key, (SUBJECTS, SLABS, SLABS), (CAP + 1) // 2, CAP + 1)
    full_dest = jax.random.randint(full_key, (SUBJECTS,), 0, SLABS)
    destination = jnp.arange(SLABS)
    return jnp.where(destination[None, None, :] == full_dest[:, None, None], CAP, counts)


def draw_send_rows(key, part):
    return jax.random.randint(jax.random.fold_in(key, 23), (SUBJECTS, SLABS, SLABS, CAP), 0, ROWS).astype(jnp.int32)


def draw_ref_slot(key, part):
    counts = pair_counts(key)
    owner_key, slot_key = jax.random.split(jax.random.fold_in(key, 37))
    owners = jax.random.randint(owner_key, (SUBJECTS, NR, NB), 0, SLABS)
    destination = (jnp.arange(NR) // ROWS)[None, :, None]
    subject_ids = jnp.arange(SUBJECTS)[:, None, None]
    limits = counts[subject_ids, owners, destination]
    within = jax.random.randint(slot_key, (SUBJECTS, NR, NB), 0, limits)
    return (owners * CAP + within).astype(jnp.int32)


def draw_columns(key, part):
    offsets = jax.random.randint(jax.random.fold_in(key, 53), (SUBJECTS, NR, NB, W), -2, 3)
    cells = jnp.arange(W, dtype=jnp.int32)
    return jnp.clip(cells + offsets, 0, W - 1).astype(jnp.int32)


def level_of(rng, shape, pieces, low, top_value):
    loudness = 1.0
    for axis_at, parts in pieces:
        draws = jax.random.uniform(jax.random.fold_in(jax.random.fold_in(rng, 6), axis_at), (parts,), jnp.float32, low / len(pieces), top_value / len(pieces))
        loudness = loudness * jnp.repeat(jnp.exp(draws), shape[axis_at] // parts).reshape((-1,) + (1,) * (len(shape) - 1 - axis_at))
    return loudness


def normal_values(stream_key, dims, spread, most, shards=(), kind=jnp.bfloat16):
    result = spread * jax.random.normal(stream_key, dims, jnp.float32)
    if shards:
        result = result * level_of(stream_key, dims, shards, -0.22, 0.18)
    return jnp.clip(result, -most, most).astype(kind)


def setup_inputs(seed: int = 0) -> dict:
    keys = jax.random.split(jax.random.key(seed), 9)
    return {
        "template": normal_values(keys[0], (NR, W), 1.0, 6.0, ((0, 16),), jnp.float32),
        "images": normal_values(keys[1], (SUBJECTS, NR, W), 1.0, 6.0, ((0, 16), (1, 16)), jnp.float32),
        "velocity": normal_values(keys[2], (SUBJECTS, 3, NR, W), 1.0, 6.0, ((0, 16), (2, 16)), jnp.float32),
        "stiffness": jnp.clip(jnp.exp(math.log(1.0) - 2.3025851 * jax.random.uniform(keys[3], (NR, W), jnp.float32) ** level_of(keys[3], (NR, W), ((0, 16),), -0.2, 0.2)), 0.1, 1.0),
        "send_rows": draw_send_rows(jax.random.fold_in(keys[8], 71), 0),
        "ref_slot": draw_ref_slot(jax.random.fold_in(keys[8], 71), 0),
        "columns": draw_columns(jax.random.fold_in(keys[8], 71), 0),
        "weights": jnp.clip(0.25 * jax.random.uniform(keys[7], (SUBJECTS, NR, NB, W), jnp.float32) ** level_of(keys[7], (SUBJECTS, NR, NB, W), ((0, 16), (1, 16)), -0.2, 0.2), 0.0, 0.25).astype(jnp.bfloat16),
    }


force_step = 1.0
diffusion_dt = 0.16
template_rate = 2.0


def central_slopes(grid_field):
    padded = jnp.pad(grid_field, 1)
    along_x = 0.5 * (padded[1:-1, 1:-1, 2:] - padded[1:-1, 1:-1, :-2])
    along_y = 0.5 * (padded[1:-1, 2:, 1:-1] - padded[1:-1, :-2, 1:-1])
    along_z = 0.5 * (padded[2:, 1:-1, 1:-1] - padded[:-2, 1:-1, 1:-1])
    return jnp.stack([along_x, along_y, along_z])


def smooth_step(field_padded, coef_padded):
    center = field_padded[:, 1:-1]
    coef_center = coef_padded[1:-1]
    field_yx = jnp.pad(center, ((0, 0), (0, 0), (1, 1), (1, 1)))
    coef_yx = jnp.pad(coef_center, ((0, 0), (1, 1), (1, 1)))
    pairs = [
        (field_padded[:, 2:], coef_padded[2:]),
        (field_padded[:, :-2], coef_padded[:-2]),
        (field_yx[:, :, 2:, 1:-1], coef_yx[:, 2:, 1:-1]),
        (field_yx[:, :, :-2, 1:-1], coef_yx[:, :-2, 1:-1]),
        (field_yx[:, :, 1:-1, 2:], coef_yx[:, 1:-1, 2:]),
        (field_yx[:, :, 1:-1, :-2], coef_yx[:, 1:-1, :-2]),
    ]
    summed = jnp.zeros(center.shape, jnp.float32)
    for neighbour, coef_near in pairs:
        face_coef = 0.5 * (coef_center + coef_near)
        summed = summed + face_coef[None] * (neighbour - center)
    return center + diffusion_dt * summed


def reference(template, images, velocity, stiffness, send_rows, ref_slot, columns, weights):
    depth_all = SLABS * PLANES
    owner_base = (jnp.arange(SLABS) * ROWS).astype(jnp.int32)
    dest_base = ((jnp.arange(NR) // ROWS) * (SLABS * CAP)).astype(jnp.int32)
    coef_grid = jnp.pad(stiffness.reshape(depth_all, YR, W), ((1, 1), (0, 0), (0, 0)))

    def per_subject(inputs):
        image_one, velocity_one, send_one, slot_one, columns_one, weights_one = inputs
        global_rows = owner_base[:, None, None] + send_one
        buffers = jnp.transpose(template[global_rows], (1, 0, 2, 3)).reshape(SLABS * SLABS * CAP, W)
        slot_global = dest_base[:, None] + slot_one
        picked = buffers[slot_global]
        values = jnp.take_along_axis(picked, columns_one, axis=2)
        weight_f = weights_one.astype(jnp.float32)
        warped = jnp.sum(weight_f * values, axis=1)
        mismatch = warped - image_one
        contrib = weight_f * mismatch[:, None, :]
        flat_index = (slot_global * W)[:, :, None] + columns_one
        slot_grad = jnp.zeros((SLABS * SLABS * CAP * W,), jnp.float32).at[flat_index.reshape(-1)].add(contrib.reshape(-1))
        slot_grad = jnp.transpose(slot_grad.reshape(SLABS, SLABS, CAP, W), (1, 0, 2, 3)).reshape(-1, W)
        row_grad = jnp.zeros((NR, W), jnp.float32).at[global_rows.reshape(-1)].add(slot_grad)
        slopes = central_slopes(warped.reshape(depth_all, YR, W))
        field = velocity_one.reshape(3, depth_all, YR, W) - force_step * mismatch.reshape(depth_all, YR, W)[None] * slopes
        for repeat in range(SMOOTH):
            field = smooth_step(jnp.pad(field, ((0, 0), (1, 1), (0, 0), (0, 0))), coef_grid)
        return row_grad, field.reshape(3, NR, W)

    row_grads, fields = lax.map(per_subject, (images, velocity, send_rows, ref_slot, columns, weights))
    template_out = template - template_rate * jnp.sum(row_grads, axis=0) / SUBJECTS
    return template_out, fields
```

```python
import functools

import jax
import jax.numpy as jnp
from jax import lax
from jax.experimental import pallas as pl
from jax.experimental.pallas import tpu as pltpu
from jax.sharding import PartitionSpec as P

YR = 256
NB = 8
HALF_DT = 0.5 * 0.16
FORCE = 1.0
RATE = 2.0
OFFSETS = (-2, -1, 0, 1, 2)
BF = jnp.bfloat16
F32 = jnp.float32


def halves(x):
    hi = x.astype(BF)
    lo = (x - hi.astype(F32)).astype(BF)
    return hi, lo


def far_first(n):
    return sorted(range(1, n), key=lambda d: -min(d, n - d))


def kernel(
    subjects, slabs, cap,
    tmpl, img, vel, stiff, send, slot_t, cols, wts,
    tout, vout,
    tmpl_v, img_v, vel_v, send_v, slot_v, cols_v, wts_v, w32, colb, wb, wd, oh, oht, os, ost,
    outbox, inbox, t2, warp, mis, place, grad, retbox, rowg, subbox, tnew, coef, stif, field, field1, field2,
    load_sem, a_send, a_recv, b_send, b_recv, c_send, c_recv, d_send, d_recv, h_send, h_recv,
):
    rows, width = tmpl_v.shape
    slots = slabs * cap
    part = rows // subjects
    me_s = lax.axis_index("subj")
    me_k = lax.axis_index("slab")

    pairs = (
        (send, send_v), (tmpl, tmpl_v), (slot_t, slot_v), (cols, cols_v), (wts, wts_v),
        (stiff, stif.at[pl.ds(2 * YR, rows), :]), (img, img_v), (vel, vel_v),
    )
    loads = [pltpu.make_async_copy(a, b, load_sem.at[i]) for i, (a, b) in enumerate(pairs)]
    for load in loads:
        load.start()

    barrier = pltpu.get_barrier_semaphore()
    for d in range(1, slabs):
        pl.semaphore_signal(barrier, inc=1, device_id={"slab": lax.rem(me_k + d, slabs)})
    for d in range(1, subjects):
        pl.semaphore_signal(barrier, inc=1, device_id={"subj": lax.rem(me_s + d, subjects)})

    def peers(axis, n, me, src, dst, send_sem, recv_sem):
        out = []
        for d in far_first(n):
            to = lax.rem(me + d, n)
            come = lax.rem(me + n - d, n)
            go = pltpu.make_async_remote_copy(
                src_ref=src(to), dst_ref=dst(me), send_sem=send_sem.at[to], recv_sem=recv_sem.at[me],
                device_id={axis: to},
            )
            got = pltpu.make_async_remote_copy(
                src_ref=src(to), dst_ref=dst(come), send_sem=send_sem.at[to], recv_sem=recv_sem.at[come],
                device_id={axis: to},
            )
            out.append((go, got))
        return out

    loads[0].wait()
    send_c = jnp.transpose(send_v[0, 0])
    lane_r = lax.broadcasted_iota(jnp.int32, (cap, rows), 1)
    for j in range(slabs):
        os[pl.ds(j * cap, cap), :] = jnp.where(send_c[:, j : j + 1] == lane_r, 1.0, 0.0).astype(BF)
    loads[1].wait()
    hi, lo = halves(tmpl_v[...])
    both = jnp.dot(os[...], jnp.concatenate([hi, lo], axis=1), preferred_element_type=F32)
    outbox[...] = both[:, :width] + both[:, width:]

    pl.semaphore_wait(barrier, slabs - 1 + subjects - 1)
    first = peers(
        "slab", slabs, me_k,
        lambda j: outbox.at[pl.ds(j * cap, cap), :], lambda k: inbox.at[pl.ds(k * cap, cap), :], a_send, a_recv,
    )
    for go, _ in first:
        go.start()
    own = pl.ds(pl.multiple_of(me_k * cap, cap), cap)
    inbox[own, :] = outbox[own, :]

    loads[2].wait()
    slot_c = jnp.transpose(slot_v[0])
    lane_q = lax.broadcasted_iota(jnp.int32, (rows, slots), 1)
    sub_q = lax.broadcasted_iota(jnp.int32, (slots, rows), 0)
    for b in range(NB):
        oh[b] = jnp.where(slot_c[:, b : b + 1] == lane_q, 1.0, 0.0).astype(BF)
        oht[b] = jnp.where(sub_q == slot_v[0, b : b + 1, :], 1.0, 0.0).astype(BF)
    ost[...] = jnp.transpose(os[...].astype(F32)).astype(BF)
    loads[3].wait()
    loads[4].wait()
    w32[...] = wts_v[...].astype(F32)
    lane = lax.broadcasted_iota(jnp.int32, (rows, width), 1)
    for b in range(NB):
        col = cols_v[pl.ds(b, rows, stride=NB), :]
        wgt = w32[pl.ds(b, rows, stride=NB), :]
        colb[b] = col
        wb[b] = wgt
        off = col - lane
        for n, d in enumerate(OFFSETS):
            kept = jnp.where(off == d, wgt, 0.0)
            wd[b, n] = pltpu.roll(kept, d % width, 1) if d else kept

    for _, got in first:
        got.wait_recv()
    hi, lo = halves(inbox[...])
    t2[:, :width] = hi
    t2[:, width:] = lo
    warp[pl.ds(YR, rows), :] = jnp.zeros((rows, width), F32)

    @pl.loop(0, NB)
    def _(b):
        both = jnp.dot(oh[b], t2[...], preferred_element_type=F32)
        picked = both[:, :width] + both[:, width:]
        values = jnp.take_along_axis(picked, colb[b], axis=1, mode="promise_in_bounds")
        warp[pl.ds(YR, rows), :] += wb[b] * values

    low = lax.rem(me_k + slabs - 1, slabs)
    high = lax.rem(me_k + 1, slabs)

    def halo(ref, lead, depth, i):
        inner = rows
        at = lambda start: ref.at[lead + (pl.ds(start, depth), slice(None))]
        base = depth
        down = pltpu.make_async_remote_copy(
            src_ref=at(base), dst_ref=at(base + inner), send_sem=h_send.at[i], recv_sem=h_recv.at[i],
            device_id={"slab": low},
        )
        up = pltpu.make_async_remote_copy(
            src_ref=at(base + inner - depth), dst_ref=at(0), send_sem=h_send.at[i + 1], recv_sem=h_recv.at[i + 1],
            device_id={"slab": high},
        )
        return down, up

    def halo_start(h):
        pl.when(me_k > 0)(h[0].start)
        pl.when(me_k < slabs - 1)(h[1].start)

    def halo_got(h):
        pl.when(me_k < slabs - 1)(h[0].wait_recv)
        pl.when(me_k > 0)(h[1].wait_recv)

    def halo_sent(h):
        pl.when(me_k > 0)(h[0].wait_send)
        pl.when(me_k < slabs - 1)(h[1].wait_send)

    @pl.when(me_k == 0)
    def _():
        warp[pl.ds(0, YR), :] = jnp.zeros((YR, width), F32)
        stif[pl.ds(0, 2 * YR), :] = jnp.zeros((2 * YR, width), F32)
        field[:, pl.ds(0, 2 * YR), :] = jnp.zeros((3, 2 * YR, width), F32)

    @pl.when(me_k == slabs - 1)
    def _():
        warp[pl.ds(YR + rows, YR), :] = jnp.zeros((YR, width), F32)
        stif[pl.ds(2 * YR + rows, 2 * YR), :] = jnp.zeros((2 * YR, width), F32)
        field[:, pl.ds(2 * YR + rows, 2 * YR), :] = jnp.zeros((3, 2 * YR, width), F32)

    warp_halo = halo(warp, (), YR, 0)
    stif_halo = halo(stif, (), 2 * YR, 2)
    field_halo = [halo(field, (a,), 2 * YR, 4 + 2 * a) for a in range(3)]
    halo_start(warp_halo)
    loads[5].wait()
    halo_start(stif_halo)

    loads[6].wait()
    mis[2] = warp[pl.ds(YR, rows), :] - img_v[0]
    for n, d in enumerate(OFFSETS):
        if d:
            mis[n] = pltpu.roll(mis[2], d % width, 1)
    grad[...] = jnp.zeros((slots, 2 * width), F32)

    @pl.loop(0, NB)
    def _(b):
        total = wd[b, 0] * mis[0]
        for n in range(1, len(OFFSETS)):
            total = total + wd[b, n] * mis[n]
        hi, lo = halves(total)
        place[:, :width] = hi
        place[:, width:] = lo
        grad[...] += jnp.dot(oht[b], place[...], preferred_element_type=F32)

    for go, _ in first:
        go.wait_send()
    outbox[...] = grad[:, :width] + grad[:, width:]
    second = peers(
        "slab", slabs, me_k,
        lambda j: outbox.at[pl.ds(j * cap, cap), :], lambda k: retbox.at[pl.ds(k * cap, cap), :], b_send, b_recv,
    )
    for go, _ in second:
        go.start()
    retbox[own, :] = outbox[own, :]

    halo_got(warp_halo)
    loads[7].wait()
    lane_p = lax.broadcasted_iota(jnp.int32, (YR, width), 1)
    row_p = lax.broadcasted_iota(jnp.int32, (YR, width), 0)

    def shifted(x):
        left = jnp.where(lane_p == 0, 0.0, pltpu.roll(x, 1, 1))
        right = jnp.where(lane_p == width - 1, 0.0, pltpu.roll(x, width - 1, 1))
        above = jnp.where(row_p == 0, 0.0, pltpu.roll(x, 1, 0))
        below = jnp.where(row_p == YR - 1, 0.0, pltpu.roll(x, YR - 1, 0))
        return left, right, above, below

    @pl.loop(0, rows // YR)
    def _(p):
        here = pl.ds(pl.multiple_of(p * YR, YR), YR)
        left, right, above, below = shifted(warp[pl.ds(pl.multiple_of((p + 1) * YR, YR), YR), :])
        before = warp[here, :]
        after = warp[pl.ds(pl.multiple_of((p + 2) * YR, YR), YR), :]
        force = (0.5 * FORCE) * mis[2, here, :]
        there = pl.ds(pl.multiple_of((p + 2) * YR, YR), YR)
        field[0, there, :] = vel_v[0, 0, here, :] - force * (right - left)
        field[1, there, :] = vel_v[0, 1, here, :] - force * (below - above)
        field[2, there, :] = vel_v[0, 2, here, :] - force * (after - before)

    for h in field_halo:
        halo_start(h)

    halo_got(stif_halo)

    @pl.loop(0, rows // YR + 2)
    def _(p):
        plane = me_k * (rows // YR) + p
        inside = jnp.where(jnp.logical_and(plane >= 1, plane <= slabs * (rows // YR)), 1.0, 0.0)
        here = pl.ds(pl.multiple_of(p * YR, YR), YR)
        centre = stif[pl.ds(pl.multiple_of((p + 1) * YR, YR), YR), :]
        before = stif[here, :]
        after = stif[pl.ds(pl.multiple_of((p + 2) * YR, YR), YR), :]
        near = shifted(centre)
        scale = inside * HALF_DT
        edges = (lane_p == 0, lane_p == width - 1, row_p == 0, row_p == YR - 1)
        spent = 6.0 * centre + before + after
        for n in range(4):
            coef[n, here, :] = jnp.where(edges[n], 0.0, scale * (centre + near[n]))
            spent = spent + near[n]
        coef[4, here, :] = scale * (centre + before)
        coef[5, here, :] = scale * (centre + after)
        coef[6, here, :] = inside - scale * spent

    for _, got in second:
        got.wait_recv()
    hi, lo = halves(retbox[...])
    both = jnp.dot(ost[...], jnp.concatenate([hi, lo], axis=1), preferred_element_type=F32)
    rowg[...] = both[:, :width] + both[:, width:]
    third = peers(
        "subj", subjects, me_s,
        lambda s: rowg.at[pl.ds(s * part, part), :], lambda s: subbox.at[pl.ds(s * part, part), :], c_send, c_recv,
    )
    for go, _ in third:
        go.start()
    mine = pl.ds(pl.multiple_of(me_s * part, part), part)
    subbox[mine, :] = rowg[mine, :]

    for _, got in third:
        got.wait_recv()
    total = subbox[pl.ds(0, part), :]
    for s in range(1, subjects):
        total = total + subbox[pl.ds(s * part, part), :]
    tnew[mine, :] = tmpl_v[mine, :] - (RATE / subjects) * total
    fourth = peers(
        "subj", subjects, me_s,
        lambda s: tnew.at[mine, :], lambda s: tnew.at[pl.ds(pl.multiple_of(s * part, part), part), :], d_send, d_recv,
    )
    for go, _ in fourth:
        go.start()

    def step(src, lead, p, q):
        at = lambda i: pl.ds(pl.multiple_of(i * YR, YR), YR)
        x = src[lead, at(p), :]
        c = lambda n: coef[n, at(q), :]
        out = c(6) * x
        out = out + c(0) * pltpu.roll(x, 1, 1)
        out = out + c(1) * pltpu.roll(x, width - 1, 1)
        out = out + c(2) * pltpu.roll(x, 1, 0)
        out = out + c(3) * pltpu.roll(x, YR - 1, 0)
        out = out + c(4) * src[lead, at(p - 1), :]
        return out + c(5) * src[lead, at(p + 1), :]

    stores = []
    for a in range(3):
        halo_got(field_halo[a])

        @pl.loop(0, rows // YR + 2)
        def _(p):
            field1[a, pl.ds(pl.multiple_of(p * YR, YR), YR), :] = step(field, a, p + 1, p)

        @pl.loop(0, rows // YR)
        def _(p):
            field2[a, pl.ds(pl.multiple_of(p * YR, YR), YR), :] = step(field1, a, p + 1, p + 1)

        stores.append(pltpu.make_async_copy(field2.at[a], vout.at[0, a], load_sem.at[a]))
        stores[-1].start()

    for _, got in fourth:
        got.wait_recv()
    stores.append(pltpu.make_async_copy(tnew, tout, load_sem.at[3]))
    stores[-1].start()
    for group in (second, third, fourth):
        for go, _ in group:
            go.wait_send()
    for h in (warp_halo, stif_halo, *field_halo):
        halo_sent(h)
    for store in stores:
        store.wait()


def per_device(subjects, slabs, template, images, velocity, stiffness, send_rows, ref_slot, columns, weights):
    rows, width = template.shape
    cap = send_rows.shape[3]
    slots = slabs * cap
    planes = rows // YR
    any_space = pl.BlockSpec(memory_space=pl.ANY)
    dma = pltpu.SemaphoreType.DMA
    vm = pltpu.VMEM
    scratch = [
        vm((rows, width), F32),
        vm((1, rows, width), F32),
        vm((1, 3, rows, width), F32),
        vm((1, 1, slabs, cap), jnp.int32),
        vm((1, NB, rows), jnp.int32),
        vm((rows * NB, width), jnp.int32),
        vm((rows * NB, width), BF),
        vm((rows * NB, width), F32),
        vm((NB, rows, width), jnp.int32),
        vm((NB, rows, width), F32),
        vm((NB, len(OFFSETS), rows, width), F32),
        vm((NB, rows, slots), BF),
        vm((NB, slots, rows), BF),
        vm((slots, rows), BF),
        vm((rows, slots), BF),
        vm((slots, width), F32),
        vm((slots, width), F32),
        vm((slots, 2 * width), BF),
        vm((rows + 2 * YR, width), F32),
        vm((len(OFFSETS), rows, width), F32),
        vm((rows, 2 * width), BF),
        vm((slots, 2 * width), F32),
        vm((slots, width), F32),
        vm((rows, width), F32),
        vm((rows, width), F32),
        vm((rows, width), F32),
        vm((7, rows + 2 * YR, width), F32),
        vm((rows + 4 * YR, width), F32),
        vm((3, rows + 4 * YR, width), F32),
        vm((3, rows + 2 * YR, width), F32),
        vm((3, rows, width), F32),
        dma((8,)),
        dma((slabs,)), dma((slabs,)), dma((slabs,)), dma((slabs,)),
        dma((subjects,)), dma((subjects,)), dma((subjects,)), dma((subjects,)),
        dma((10,)), dma((10,)),
    ]
    return pl.pallas_call(
        functools.partial(kernel, subjects, slabs, cap),
        out_shape=(
            jax.ShapeDtypeStruct((rows, width), F32),
            jax.ShapeDtypeStruct((1, 3, rows, width), F32),
        ),
        in_specs=[any_space] * 8,
        out_specs=(any_space, any_space),
        scratch_shapes=scratch,
        compiler_params=pltpu.CompilerParams(
            collective_id=0, has_side_effects=True, vmem_limit_bytes=56 * 2**20
        ),
    )(
        template, images, velocity, stiffness, send_rows,
        jnp.transpose(ref_slot, (0, 2, 1)),
        columns.reshape(rows * NB, width),
        weights.reshape(rows * NB, width),
    )


def solution(mesh):
    return jax.shard_map(
        functools.partial(per_device, mesh.shape["subj"], mesh.shape["slab"]),
        mesh=mesh,
        in_specs=(
            P("slab", None),
            P("subj", "slab", None),
            P("subj", None, "slab", None),
            P("slab", None),
            P("subj", "slab", None, None),
            P("subj", "slab", None),
            P("subj", "slab", None, None),
            P("subj", "slab", None, None),
        ),
        out_specs=(P("slab", None), P("subj", None, "slab", None)),
        check_vma=False,
    )
```

```python
import functools

import jax
import jax.numpy as jnp
from jax import lax
from jax.experimental import pallas as pl
from jax.experimental.pallas import tpu as pltpu
from jax.sharding import PartitionSpec as P

YR = 256
NB = 8
HALF_DT = 0.5 * 0.16
FORCE = 1.0
RATE = 2.0
OFFSETS = (-2, -1, 0, 1, 2)
BF = jnp.bfloat16
F32 = jnp.float32


def halves(x):
    hi = x.astype(BF)
    lo = (x - hi.astype(F32)).astype(BF)
    return hi, lo


def far_first(n):
    return sorted(range(1, n), key=lambda d: -min(d, n - d))


def kernel(
    subjects, slabs, cap,
    tmpl, img, vel, stiff, send, slot_t, cols, wts,
    tout, vout,
    tmpl_v, img_v, vel_v, send_v, slot_v, cols_v, wts_v, w32, colb, wb, wd, oh, oht, os, ost,
    outbox, inbox, t2, warp, mis, place, retbox, rowg, subbox, coef, stif, field, field1,
    load_sem, a_send, a_recv, b_send, b_recv, c_send, c_recv, d_send, d_recv, e_send, e_recv, h_send, h_recv,
):
    rows, width = tmpl_v.shape
    slots = slabs * cap
    part = rows // subjects
    me_s = lax.axis_index("subj")
    me_k = lax.axis_index("slab")

    pairs = (
        (send, send_v), (tmpl, tmpl_v), (slot_t, slot_v), (cols, cols_v), (wts, wts_v),
        (stiff, stif.at[pl.ds(2 * YR, rows), :]), (img, img_v), (vel, vel_v),
    )
    loads = [pltpu.make_async_copy(a, b, load_sem.at[i]) for i, (a, b) in enumerate(pairs)]
    for load in loads:
        load.start()

    barrier = pltpu.get_barrier_semaphore()
    for d in range(1, slabs):
        pl.semaphore_signal(barrier, inc=1, device_id={"slab": lax.rem(me_k + d, slabs)})
    for d in range(1, subjects):
        pl.semaphore_signal(barrier, inc=1, device_id={"subj": lax.rem(me_s + d, subjects)})

    def peers(axis, n, me, src, dst, send_sem, recv_sem):
        out = []
        for d in far_first(n):
            to = lax.rem(me + d, n)
            come = lax.rem(me + n - d, n)
            go = pltpu.make_async_remote_copy(
                src_ref=src(to), dst_ref=dst(me), send_sem=send_sem.at[to], recv_sem=recv_sem.at[me],
                device_id={axis: to},
            )
            got = pltpu.make_async_remote_copy(
                src_ref=src(to), dst_ref=dst(come), send_sem=send_sem.at[to], recv_sem=recv_sem.at[come],
                device_id={axis: to},
            )
            out.append((go, got))
        return out

    loads[0].wait()
    send_c = jnp.transpose(send_v[0, 0])
    lane_r = lax.broadcasted_iota(jnp.int32, (cap, rows), 1)
    for j in range(slabs):
        os[pl.ds(j * cap, cap), :] = jnp.where(send_c[:, j : j + 1] == lane_r, 1.0, 0.0).astype(BF)
    loads[1].wait()
    hi, lo = halves(tmpl_v[...])
    both = jnp.dot(os[...], jnp.concatenate([hi, lo], axis=1), preferred_element_type=F32)
    outbox[...] = both[:, :width] + both[:, width:]

    odd = lax.rem(me_k, 2)
    other = me_k + 1 - 2 * odd
    across = me_k - 1 + 2 * odd
    linked = jnp.logical_and(across >= 0, across < slabs)
    mine = pl.ds(pl.multiple_of(me_s * part, part), part)
    low_at, own_at, high_at = 0, 2 * YR, 2 * YR + rows
    far_in = low_at + odd * (high_at - low_at)
    far_out = high_at - odd * (high_at - low_at)
    stif_near = pltpu.make_async_remote_copy(
        src_ref=stif.at[pl.ds(own_at, rows), :], dst_ref=stif.at[pl.ds(pl.multiple_of(far_in, rows), rows), :],
        send_sem=h_send.at[2], recv_sem=h_recv.at[2], device_id={"slab": other},
    )

    def stif_rows(start):
        return stif.at[pl.ds(pl.multiple_of(start, part), part), :]

    stif_far = pltpu.make_async_remote_copy(
        src_ref=stif_rows(own_at + me_s * part), dst_ref=stif_rows(far_out + me_s * part),
        send_sem=h_send.at[3], recv_sem=h_recv.at[3], device_id={"slab": jnp.clip(across, 0, slabs - 1)},
    )
    loads[5].wait()

    pl.semaphore_wait(barrier, slabs - 1 + subjects - 1)
    pl.when(linked)(stif_far.start)
    first = peers(
        "slab", slabs, me_k,
        lambda j: outbox.at[pl.ds(j * cap, cap), :], lambda k: inbox.at[pl.ds(k * cap, cap), :], a_send, a_recv,
    )
    for go, _ in first:
        go.start()
    own = pl.ds(pl.multiple_of(me_k * cap, cap), cap)
    inbox[own, :] = outbox[own, :]

    stif_near.start()

    loads[2].wait()
    slot_c = jnp.transpose(slot_v[0])
    lane_q = lax.broadcasted_iota(jnp.int32, (rows, slots), 1)
    sub_q = lax.broadcasted_iota(jnp.int32, (slots, rows), 0)
    for b in range(NB):
        oh[b] = jnp.where(slot_c[:, b : b + 1] == lane_q, 1.0, 0.0).astype(BF)
        oht[:, pl.ds(b * rows, rows)] = jnp.where(sub_q == slot_v[0, b : b + 1, :], 1.0, 0.0).astype(BF)
    ost[...] = jnp.transpose(os[...].astype(F32)).astype(BF)
    loads[3].wait()
    loads[4].wait()
    w32[...] = wts_v[...].astype(F32)
    lane = lax.broadcasted_iota(jnp.int32, (rows, width), 1)
    for b in range(NB):
        col = cols_v[pl.ds(b, rows, stride=NB), :]
        wgt = w32[pl.ds(b, rows, stride=NB), :]
        colb[b] = col
        wb[b] = wgt
        off = col - lane
        for n, d in enumerate(OFFSETS):
            kept = jnp.where(off == d, wgt, 0.0)
            wd[b, n] = pltpu.roll(kept, d % width, 1) if d else kept

    shared = peers(
        "subj", subjects, me_s,
        lambda s: stif_rows(far_in + me_s * part), lambda s: stif_rows(far_in + s * part), e_send, e_recv,
    )

    @pl.when(linked)
    def _():
        stif_far.wait_recv()
        for go, _ in shared:
            go.start()

    for _, got in first:
        got.wait_recv()
    hi, lo = halves(inbox[...])
    t2[:, :width] = hi
    t2[:, width:] = lo
    block = rows // 2
    for c in range(2):
        here = pl.ds(c * block, block)
        total = None
        for b in range(NB):
            both = jnp.dot(oh[b, here, :], t2[...], preferred_element_type=F32)
            picked = both[:, :width] + both[:, width:]
            values = jnp.take_along_axis(picked, colb[b, here, :], axis=1, mode="promise_in_bounds")
            term = wb[b, here, :] * values
            total = term if total is None else total + term
        warp[pl.ds(YR + c * block, block), :] = total

    low = lax.rem(me_k + slabs - 1, slabs)
    high = lax.rem(me_k + 1, slabs)

    def halo(ref, lead, depth, i):
        inner = rows
        at = lambda start: ref.at[lead + (pl.ds(start, depth), slice(None))]
        base = depth
        down = pltpu.make_async_remote_copy(
            src_ref=at(base), dst_ref=at(base + inner), send_sem=h_send.at[i], recv_sem=h_recv.at[i],
            device_id={"slab": low},
        )
        up = pltpu.make_async_remote_copy(
            src_ref=at(base + inner - depth), dst_ref=at(0), send_sem=h_send.at[i + 1], recv_sem=h_recv.at[i + 1],
            device_id={"slab": high},
        )
        return down, up

    def halo_start(h):
        pl.when(me_k > 0)(h[0].start)
        pl.when(me_k < slabs - 1)(h[1].start)

    def halo_got(h):
        pl.when(me_k < slabs - 1)(h[0].wait_recv)
        pl.when(me_k > 0)(h[1].wait_recv)

    def halo_sent(h):
        pl.when(me_k > 0)(h[0].wait_send)
        pl.when(me_k < slabs - 1)(h[1].wait_send)

    @pl.when(me_k == 0)
    def _():
        warp[pl.ds(0, YR), :] = jnp.zeros((YR, width), F32)
        stif[pl.ds(0, 2 * YR), :] = jnp.zeros((2 * YR, width), F32)
        field[:, pl.ds(0, 2 * YR), :] = jnp.zeros((3, 2 * YR, width), F32)

    @pl.when(me_k == slabs - 1)
    def _():
        warp[pl.ds(YR + rows, YR), :] = jnp.zeros((YR, width), F32)
        stif[pl.ds(2 * YR + rows, 2 * YR), :] = jnp.zeros((2 * YR, width), F32)
        field[:, pl.ds(2 * YR + rows, 2 * YR), :] = jnp.zeros((3, 2 * YR, width), F32)

    warp_halo = halo(warp, (), YR, 0)
    field_halo = [halo(field, (a,), 2 * YR, 4 + 2 * a) for a in range(3)]
    halo_start(warp_halo)

    loads[6].wait()
    mis[2] = warp[pl.ds(YR, rows), :] - img_v[0]
    for n, d in enumerate(OFFSETS):
        if d:
            mis[n] = pltpu.roll(mis[2], d % width, 1)
    block = rows // 8
    for b in range(NB):
        for c in range(8):
            here = pl.ds(c * block, block)
            total = wd[b, 0, here, :] * mis[0, here, :]
            for n in range(1, len(OFFSETS)):
                total = total + wd[b, n, here, :] * mis[n, here, :]
            hi, lo = halves(total)
            place[pl.ds(b * rows + c * block, block), :width] = hi
            place[pl.ds(b * rows + c * block, block), width:] = lo
    both = jnp.dot(oht[...], place[...], preferred_element_type=F32)

    for go, _ in first:
        go.wait_send()
    outbox[...] = both[:, :width] + both[:, width:]
    second = peers(
        "slab", slabs, me_k,
        lambda j: outbox.at[pl.ds(j * cap, cap), :], lambda k: retbox.at[pl.ds(k * cap, cap), :], b_send, b_recv,
    )
    for go, _ in second:
        go.start()
    retbox[own, :] = outbox[own, :]

    halo_got(warp_halo)
    loads[7].wait()
    lane_p = lax.broadcasted_iota(jnp.int32, (YR, width), 1)
    row_p = lax.broadcasted_iota(jnp.int32, (YR, width), 0)

    def shifted(x):
        left = jnp.where(lane_p == 0, 0.0, pltpu.roll(x, 1, 1))
        right = jnp.where(lane_p == width - 1, 0.0, pltpu.roll(x, width - 1, 1))
        above = jnp.where(row_p == 0, 0.0, pltpu.roll(x, 1, 0))
        below = jnp.where(row_p == YR - 1, 0.0, pltpu.roll(x, YR - 1, 0))
        return left, right, above, below

    @pl.loop(0, rows // YR)
    def _(p):
        here = pl.ds(pl.multiple_of(p * YR, YR), YR)
        left, right, above, below = shifted(warp[pl.ds(pl.multiple_of((p + 1) * YR, YR), YR), :])
        before = warp[here, :]
        after = warp[pl.ds(pl.multiple_of((p + 2) * YR, YR), YR), :]
        force = (0.5 * FORCE) * mis[2, here, :]
        there = pl.ds(pl.multiple_of((p + 2) * YR, YR), YR)
        field[0, there, :] = vel_v[0, 0, here, :] - force * (right - left)
        field[1, there, :] = vel_v[0, 1, here, :] - force * (below - above)
        field[2, there, :] = vel_v[0, 2, here, :] - force * (after - before)

    for h in field_halo:
        halo_start(h)

    stif_near.wait_recv()

    @pl.when(linked)
    def _():
        for _, got in shared:
            got.wait_recv()

    @pl.loop(0, rows // YR + 2)
    def _(p):
        plane = me_k * (rows // YR) + p
        inside = jnp.where(jnp.logical_and(plane >= 1, plane <= slabs * (rows // YR)), 1.0, 0.0)
        here = pl.ds(pl.multiple_of(p * YR, YR), YR)
        centre = stif[pl.ds(pl.multiple_of((p + 1) * YR, YR), YR), :]
        before = stif[here, :]
        after = stif[pl.ds(pl.multiple_of((p + 2) * YR, YR), YR), :]
        near = shifted(centre)
        scale = inside * HALF_DT
        edges = (lane_p == 0, lane_p == width - 1, row_p == 0, row_p == YR - 1)
        spent = 6.0 * centre + before + after
        for n in range(4):
            coef[n, here, :] = jnp.where(edges[n], 0.0, scale * (centre + near[n]))
            spent = spent + near[n]
        coef[4, here, :] = scale * (centre + before)
        coef[5, here, :] = scale * (centre + after)
        coef[6, here, :] = inside - scale * spent

    for _, got in second:
        got.wait_recv()
    hi, lo = halves(retbox[...])
    both = jnp.dot(ost[...], jnp.concatenate([hi, lo], axis=1), preferred_element_type=F32)
    rowg[...] = both[:, :width] + both[:, width:]
    third = peers(
        "subj", subjects, me_s,
        lambda s: rowg.at[pl.ds(s * part, part), :], lambda s: subbox.at[pl.ds(s * part, part), :], c_send, c_recv,
    )
    for go, _ in third:
        go.start()
    subbox[mine, :] = rowg[mine, :]

    for _, got in third:
        got.wait_recv()
    total = subbox[pl.ds(0, part), :]
    for s in range(1, subjects):
        total = total + subbox[pl.ds(s * part, part), :]
    tout[mine, :] = tmpl_v[mine, :] - (RATE / subjects) * total
    fourth = peers(
        "subj", subjects, me_s,
        lambda s: tout.at[mine, :], lambda s: tout.at[pl.ds(pl.multiple_of(s * part, part), part), :], d_send, d_recv,
    )
    for go, _ in fourth:
        go.start()

    def step(src, lead, p, q):
        at = lambda i: pl.ds(pl.multiple_of(i * YR, YR), YR)
        x = src[lead, at(p), :]
        c = lambda n: coef[n, at(q), :]
        out = c(6) * x
        out = out + c(0) * pltpu.roll(x, 1, 1)
        out = out + c(1) * pltpu.roll(x, width - 1, 1)
        out = out + c(2) * pltpu.roll(x, 1, 0)
        out = out + c(3) * pltpu.roll(x, YR - 1, 0)
        out = out + c(4) * src[lead, at(p - 1), :]
        return out + c(5) * src[lead, at(p + 1), :]

    def diffuse(a):
        halo_got(field_halo[a])

        @pl.loop(0, rows // YR + 2)
        def _(p):
            field1[a, pl.ds(pl.multiple_of(p * YR, YR), YR), :] = step(field, a, p + 1, p)

        @pl.loop(0, rows // YR)
        def _(p):
            vout[0, a, pl.ds(pl.multiple_of(p * YR, YR), YR), :] = step(field1, a, p + 1, p + 1)

    for a in range(3):
        diffuse(a)

    for _, got in fourth:
        got.wait_recv()
    for group in (second, third, fourth):
        for go, _ in group:
            go.wait_send()
    for h in (warp_halo, *field_halo):
        halo_sent(h)
    stif_near.wait_send()

    @pl.when(linked)
    def _():
        stif_far.wait_send()
        for go, _ in shared:
            go.wait_send()


def store(template, velocity, tout, vout, sem):
    one = pltpu.make_async_copy(velocity, vout, sem.at[0])
    two = pltpu.make_async_copy(template, tout, sem.at[1])
    one.start()
    two.start()
    one.wait()
    two.wait()


def per_device(subjects, slabs, template, images, velocity, stiffness, send_rows, ref_slot, columns, weights):
    rows, width = template.shape
    cap = send_rows.shape[3]
    slots = slabs * cap
    planes = rows // YR
    hbm_space = pl.BlockSpec(memory_space=pltpu.HBM)
    dma = pltpu.SemaphoreType.DMA
    vm = pltpu.VMEM
    scratch = [
        vm((rows, width), F32),
        vm((1, rows, width), F32),
        vm((1, 3, rows, width), F32),
        vm((1, 1, slabs, cap), jnp.int32),
        vm((1, NB, rows), jnp.int32),
        vm((rows * NB, width), jnp.int32),
        vm((rows * NB, width), BF),
        vm((rows * NB, width), F32),
        vm((NB, rows, width), jnp.int32),
        vm((NB, rows, width), F32),
        vm((NB, len(OFFSETS), rows, width), F32),
        vm((NB, rows, slots), BF),
        vm((slots, NB * rows), BF),
        vm((slots, rows), BF),
        vm((rows, slots), BF),
        vm((slots, width), F32),
        vm((slots, width), F32),
        vm((slots, 2 * width), BF),
        vm((rows + 2 * YR, width), F32),
        vm((len(OFFSETS), rows, width), F32),
        vm((NB * rows, 2 * width), BF),
        vm((slots, width), F32),
        vm((rows, width), F32),
        vm((rows, width), F32),
        vm((7, rows + 2 * YR, width), F32),
        vm((rows + 4 * YR, width), F32),
        vm((3, rows + 4 * YR, width), F32),
        vm((3, rows + 2 * YR, width), F32),
        dma((8,)),
        dma((slabs,)), dma((slabs,)), dma((slabs,)), dma((slabs,)),
        dma((subjects,)), dma((subjects,)), dma((subjects,)), dma((subjects,)),
        dma((subjects,)), dma((subjects,)), dma((10,)), dma((10,)),
    ]
    outs = (
        jax.ShapeDtypeStruct((rows, width), F32),
        jax.ShapeDtypeStruct((1, 3, rows, width), F32),
    )
    vmem_space = pl.BlockSpec(memory_space=vm)
    new = pl.pallas_call(
        functools.partial(kernel, subjects, slabs, cap),
        out_shape=tuple(vm(o.shape, o.dtype) for o in outs),
        in_specs=[hbm_space] * 8,
        out_specs=(vmem_space, vmem_space),
        scratch_shapes=scratch,
        compiler_params=pltpu.CompilerParams(
            collective_id=0, has_side_effects=True, vmem_limit_bytes=62 * 2**20
        ),
    )(
        template, images, velocity, stiffness, send_rows,
        jnp.transpose(ref_slot, (0, 2, 1)),
        columns.reshape(rows * NB, width),
        weights.reshape(rows * NB, width),
    )
    return pl.pallas_call(
        store,
        out_shape=outs,
        in_specs=[pl.BlockSpec(memory_space=pl.ANY)] * 2,
        out_specs=(hbm_space, hbm_space),
        scratch_shapes=[dma((2,))],
        compiler_params=pltpu.CompilerParams(vmem_limit_bytes=2**20),
    )(*new)


def solution(mesh):
    return jax.shard_map(
        functools.partial(per_device, mesh.shape["subj"], mesh.shape["slab"]),
        mesh=mesh,
        in_specs=(
            P("slab", None),
            P("subj", "slab", None),
            P("subj", None, "slab", None),
            P("slab", None),
            P("subj", "slab", None, None),
            P("subj", "slab", None),
            P("subj", "slab", None, None),
            P("subj", "slab", None, None),
        ),
        out_specs=(P("slab", None), P("subj", None, "slab", None)),
        check_vma=False,
    )
```

```python
import functools
import math

import jax
import jax.numpy as jnp
from jax import lax
from jax.experimental import pallas as pl
from jax.experimental.pallas import tpu as pltpu
from jax.sharding import PartitionSpec as P

YR = 256
NB = 8
HALF_DT = 0.5 * 0.16
FORCE = 1.0
RATE = 2.0
OFFSETS = (-2, -1, 0, 1, 2)
BF = jnp.bfloat16
F32 = jnp.float32


def halves(x):
    hi = x.astype(BF)
    lo = (x - hi.astype(F32)).astype(BF)
    return hi, lo


def torus(outer, inner):
    hops = lambda d, n: min(d, n - d)
    every = [(a, b) for a in range(outer) for b in range(inner) if (a, b) != (0, 0)]
    return sorted(every, key=lambda o: -hops(o[0], outer) - hops(o[1], inner))


def shift(me, outer, inner, a, b):
    return lax.rem(me // inner + a, outer) * inner + lax.rem(lax.rem(me, inner) + b, inner)


def kernel(
    subjects, slabs, cap,
    tmpl, img, vel, stiff, send, slot_t, cols, wts,
    tout, vout,
    tmpl_v, img_v, vel_v, send_v, slot_v, cols_v, wts_v, w32, colb, wb, wd, oh, oht, os, ost,
    outbox, inbox, t2, warp, mis, place, retbox, rowg, subbox, coef, stif, field, field1,
    load_sem, a_send, a_recv, b_send, b_recv, c_send, c_recv, d_send, d_recv, e_send, e_recv, h_send, h_recv,
):
    rows, width = tmpl_v.shape
    slots = slabs * cap
    part = rows // subjects
    me_s = lax.axis_index("subj")
    me_k = lax.axis_index("slab")

    pairs = (
        (send, send_v), (tmpl, tmpl_v), (slot_t, slot_v), (cols, cols_v), (wts, wts_v),
        (stiff, stif.at[pl.ds(2 * YR, rows), :]), (img, img_v), (vel, vel_v),
    )
    loads = [pltpu.make_async_copy(a, b, load_sem.at[i]) for i, (a, b) in enumerate(pairs)]
    for load in loads[:2]:
        load.start()

    side = math.isqrt(subjects)
    shapes = {"slab": (me_k, slabs // 2, 2), "subj": (me_s, subjects // side, side)}
    barrier = pltpu.get_barrier_semaphore()
    for z, xy in zip(torus(*shapes["slab"][1:]), torus(*shapes["subj"][1:])):
        pl.semaphore_signal(barrier, inc=1, device_id={"slab": shift(*shapes["slab"], *z)})
        pl.semaphore_signal(barrier, inc=1, device_id={"subj": shift(*shapes["subj"], *xy)})
    for load in loads[2:]:
        load.start()

    def peers(axis, src, dst, send_sem, recv_sem):
        out = []
        me, outer, inner = shapes[axis]
        for a, b in torus(outer, inner):
            to = shift(me, outer, inner, a, b)
            come = shift(me, outer, inner, outer - a, inner - b)
            go = pltpu.make_async_remote_copy(
                src_ref=src(to), dst_ref=dst(me), send_sem=send_sem.at[to], recv_sem=recv_sem.at[me],
                device_id={axis: to},
            )
            got = pltpu.make_async_remote_copy(
                src_ref=src(to), dst_ref=dst(come), send_sem=send_sem.at[to], recv_sem=recv_sem.at[come],
                device_id={axis: to},
            )
            out.append((go, got))
        return out

    loads[0].wait()
    send_c = jnp.transpose(send_v[0, 0])
    lane_r = lax.broadcasted_iota(jnp.int32, (cap, rows), 1)
    for j in range(slabs):
        os[pl.ds(j * cap, cap), :] = jnp.where(send_c[:, j : j + 1] == lane_r, 1.0, 0.0).astype(BF)
    loads[1].wait()
    hi, lo = halves(tmpl_v[...])
    both = jnp.dot(os[...], jnp.concatenate([hi, lo], axis=1), preferred_element_type=F32)
    outbox[...] = both[:, :width] + both[:, width:]

    odd = lax.rem(me_k, 2)
    other = me_k + 1 - 2 * odd
    across = me_k - 1 + 2 * odd
    linked = jnp.logical_and(across >= 0, across < slabs)
    mine = pl.ds(pl.multiple_of(me_s * part, part), part)
    low_at, own_at, high_at = 0, 2 * YR, 2 * YR + rows
    far_in = low_at + odd * (high_at - low_at)
    far_out = high_at - odd * (high_at - low_at)
    stif_near = pltpu.make_async_remote_copy(
        src_ref=stif.at[pl.ds(own_at, rows), :], dst_ref=stif.at[pl.ds(pl.multiple_of(far_in, rows), rows), :],
        send_sem=h_send.at[2], recv_sem=h_recv.at[2], device_id={"slab": other},
    )

    def stif_rows(start):
        return stif.at[pl.ds(pl.multiple_of(start, part), part), :]

    stif_far = pltpu.make_async_remote_copy(
        src_ref=stif_rows(own_at + me_s * part), dst_ref=stif_rows(far_out + me_s * part),
        send_sem=h_send.at[3], recv_sem=h_recv.at[3], device_id={"slab": jnp.clip(across, 0, slabs - 1)},
    )
    loads[5].wait()

    pl.semaphore_wait(barrier, slabs - 1 + subjects - 1)
    pl.when(linked)(stif_far.start)
    first = peers(
        "slab",
        lambda j: outbox.at[pl.ds(j * cap, cap), :], lambda k: inbox.at[pl.ds(k * cap, cap), :], a_send, a_recv,
    )
    for go, _ in first:
        go.start()
    own = pl.ds(pl.multiple_of(me_k * cap, cap), cap)
    inbox[own, :] = outbox[own, :]

    stif_near.start()

    loads[2].wait()
    slot_c = jnp.transpose(slot_v[0])
    lane_q = lax.broadcasted_iota(jnp.int32, (rows, slots), 1)
    sub_q = lax.broadcasted_iota(jnp.int32, (slots, rows), 0)
    for b in range(NB):
        oh[b] = jnp.where(slot_c[:, b : b + 1] == lane_q, 1.0, 0.0).astype(BF)
        oht[:, pl.ds(b * rows, rows)] = jnp.where(sub_q == slot_v[0, b : b + 1, :], 1.0, 0.0).astype(BF)
    ost[...] = jnp.transpose(os[...].astype(F32)).astype(BF)
    loads[3].wait()
    loads[4].wait()
    w32[...] = wts_v[...].astype(F32)
    lane = lax.broadcasted_iota(jnp.int32, (rows, width), 1)
    for b in range(NB):
        col = cols_v[pl.ds(b, rows, stride=NB), :]
        wgt = w32[pl.ds(b, rows, stride=NB), :]
        colb[b] = col
        wb[b] = wgt
        off = col - lane
        for n, d in enumerate(OFFSETS):
            kept = jnp.where(off == d, wgt, 0.0)
            wd[b, n] = pltpu.roll(kept, d % width, 1) if d else kept

    shared = peers(
        "subj",
        lambda s: stif_rows(far_in + me_s * part), lambda s: stif_rows(far_in + s * part), e_send, e_recv,
    )

    @pl.when(linked)
    def _():
        stif_far.wait_recv()
        for go, _ in shared:
            go.start()

    for _, got in first:
        got.wait_recv()
    hi, lo = halves(inbox[...])
    t2[:, :width] = hi
    t2[:, width:] = lo
    block = rows // 2
    for c in range(2):
        here = pl.ds(c * block, block)
        total = None
        for b in range(NB):
            both = jnp.dot(oh[b, here, :], t2[...], preferred_element_type=F32)
            picked = both[:, :width] + both[:, width:]
            values = jnp.take_along_axis(picked, colb[b, here, :], axis=1, mode="promise_in_bounds")
            term = wb[b, here, :] * values
            total = term if total is None else total + term
        warp[pl.ds(YR + c * block, block), :] = total

    low = lax.rem(me_k + slabs - 1, slabs)
    high = lax.rem(me_k + 1, slabs)

    def halo(ref, lead, depth, i):
        inner = rows
        at = lambda start: ref.at[lead + (pl.ds(start, depth), slice(None))]
        base = depth
        down = pltpu.make_async_remote_copy(
            src_ref=at(base), dst_ref=at(base + inner), send_sem=h_send.at[i], recv_sem=h_recv.at[i],
            device_id={"slab": low},
        )
        up = pltpu.make_async_remote_copy(
            src_ref=at(base + inner - depth), dst_ref=at(0), send_sem=h_send.at[i + 1], recv_sem=h_recv.at[i + 1],
            device_id={"slab": high},
        )
        return down, up

    def halo_start(h):
        pl.when(me_k > 0)(h[0].start)
        pl.when(me_k < slabs - 1)(h[1].start)

    def halo_got(h):
        pl.when(me_k < slabs - 1)(h[0].wait_recv)
        pl.when(me_k > 0)(h[1].wait_recv)

    def halo_sent(h):
        pl.when(me_k > 0)(h[0].wait_send)
        pl.when(me_k < slabs - 1)(h[1].wait_send)

    @pl.when(me_k == 0)
    def _():
        warp[pl.ds(0, YR), :] = jnp.zeros((YR, width), F32)
        stif[pl.ds(0, 2 * YR), :] = jnp.zeros((2 * YR, width), F32)
        field[:, pl.ds(0, 2 * YR), :] = jnp.zeros((3, 2 * YR, width), F32)

    @pl.when(me_k == slabs - 1)
    def _():
        warp[pl.ds(YR + rows, YR), :] = jnp.zeros((YR, width), F32)
        stif[pl.ds(2 * YR + rows, 2 * YR), :] = jnp.zeros((2 * YR, width), F32)
        field[:, pl.ds(2 * YR + rows, 2 * YR), :] = jnp.zeros((3, 2 * YR, width), F32)

    warp_halo = halo(warp, (), YR, 0)
    field_halo = [halo(field, (a,), 2 * YR, 4 + 2 * a) for a in range(3)]
    halo_start(warp_halo)

    loads[6].wait()
    mis[2] = warp[pl.ds(YR, rows), :] - img_v[0]
    for n, d in enumerate(OFFSETS):
        if d:
            mis[n] = pltpu.roll(mis[2], d % width, 1)
    block = rows // 8
    for b in range(NB):
        for c in range(8):
            here = pl.ds(c * block, block)
            total = wd[b, 0, here, :] * mis[0, here, :]
            for n in range(1, len(OFFSETS)):
                total = total + wd[b, n, here, :] * mis[n, here, :]
            hi, lo = halves(total)
            place[pl.ds(b * rows + c * block, block), :width] = hi
            place[pl.ds(b * rows + c * block, block), width:] = lo
    for go, _ in first:
        go.wait_send()
    second = peers(
        "slab",
        lambda j: outbox.at[pl.ds(j * cap, cap), :], lambda k: retbox.at[pl.ds(k * cap, cap), :], b_send, b_recv,
    )
    for part_of in range(2):
        here = pl.ds(part_of * (slots // 2), slots // 2)
        both = jnp.dot(oht[here, :], place[...], preferred_element_type=F32)
        outbox[here, :] = both[:, :width] + both[:, width:]
        for (go, _), (a, b) in zip(second, torus(slabs // 2, 2)):
            to = shift(me_k, slabs // 2, 2, a, b)
            pl.when(to // (slabs // 2) == part_of)(go.start)
    retbox[own, :] = outbox[own, :]

    halo_got(warp_halo)
    loads[7].wait()
    lane_p = lax.broadcasted_iota(jnp.int32, (YR, width), 1)
    row_p = lax.broadcasted_iota(jnp.int32, (YR, width), 0)

    def shifted(x):
        left = jnp.where(lane_p == 0, 0.0, pltpu.roll(x, 1, 1))
        right = jnp.where(lane_p == width - 1, 0.0, pltpu.roll(x, width - 1, 1))
        above = jnp.where(row_p == 0, 0.0, pltpu.roll(x, 1, 0))
        below = jnp.where(row_p == YR - 1, 0.0, pltpu.roll(x, YR - 1, 0))
        return left, right, above, below

    @pl.loop(0, rows // YR)
    def _(p):
        here = pl.ds(pl.multiple_of(p * YR, YR), YR)
        left, right, above, below = shifted(warp[pl.ds(pl.multiple_of((p + 1) * YR, YR), YR), :])
        before = warp[here, :]
        after = warp[pl.ds(pl.multiple_of((p + 2) * YR, YR), YR), :]
        force = (0.5 * FORCE) * mis[2, here, :]
        there = pl.ds(pl.multiple_of((p + 2) * YR, YR), YR)
        field[0, there, :] = vel_v[0, 0, here, :] - force * (right - left)
        field[1, there, :] = vel_v[0, 1, here, :] - force * (below - above)
        field[2, there, :] = vel_v[0, 2, here, :] - force * (after - before)

    for h in field_halo:
        halo_start(h)

    stif_near.wait_recv()

    @pl.when(linked)
    def _():
        for _, got in shared:
            got.wait_recv()

    @pl.loop(0, rows // YR + 2)
    def _(p):
        plane = me_k * (rows // YR) + p
        inside = jnp.where(jnp.logical_and(plane >= 1, plane <= slabs * (rows // YR)), 1.0, 0.0)
        here = pl.ds(pl.multiple_of(p * YR, YR), YR)
        centre = stif[pl.ds(pl.multiple_of((p + 1) * YR, YR), YR), :]
        before = stif[here, :]
        after = stif[pl.ds(pl.multiple_of((p + 2) * YR, YR), YR), :]
        near = shifted(centre)
        scale = inside * HALF_DT
        edges = (lane_p == 0, lane_p == width - 1, row_p == 0, row_p == YR - 1)
        spent = 6.0 * centre + before + after
        for n in range(4):
            coef[n, here, :] = jnp.where(edges[n], 0.0, scale * (centre + near[n]))
            spent = spent + near[n]
        coef[4, here, :] = scale * (centre + before)
        coef[5, here, :] = scale * (centre + after)
        coef[6, here, :] = inside - scale * spent

    for _, got in second:
        got.wait_recv()
    hi, lo = halves(retbox[...])
    both = jnp.dot(ost[...], jnp.concatenate([hi, lo], axis=1), preferred_element_type=F32)
    rowg[...] = both[:, :width] + both[:, width:]
    third = peers(
        "subj",
        lambda s: rowg.at[pl.ds(s * part, part), :], lambda s: subbox.at[pl.ds(s * part, part), :], c_send, c_recv,
    )
    for go, _ in third:
        go.start()
    subbox[mine, :] = rowg[mine, :]

    for _, got in third:
        got.wait_recv()
    total = subbox[pl.ds(0, part), :]
    for s in range(1, subjects):
        total = total + subbox[pl.ds(s * part, part), :]
    tout[mine, :] = tmpl_v[mine, :] - (RATE / subjects) * total
    fourth = peers(
        "subj",
        lambda s: tout.at[mine, :], lambda s: tout.at[pl.ds(pl.multiple_of(s * part, part), part), :], d_send, d_recv,
    )
    for go, _ in fourth:
        go.start()

    def step(src, lead, p, q):
        at = lambda i: pl.ds(pl.multiple_of(i * YR, YR), YR)
        x = src[lead, at(p), :]
        c = lambda n: coef[n, at(q), :]
        out = c(6) * x
        out = out + c(0) * pltpu.roll(x, 1, 1)
        out = out + c(1) * pltpu.roll(x, width - 1, 1)
        out = out + c(2) * pltpu.roll(x, 1, 0)
        out = out + c(3) * pltpu.roll(x, YR - 1, 0)
        out = out + c(4) * src[lead, at(p - 1), :]
        return out + c(5) * src[lead, at(p + 1), :]

    def diffuse(a):
        halo_got(field_halo[a])

        @pl.loop(0, rows // YR + 2)
        def _(p):
            field1[a, pl.ds(pl.multiple_of(p * YR, YR), YR), :] = step(field, a, p + 1, p)

        @pl.loop(0, rows // YR)
        def _(p):
            vout[0, a, pl.ds(pl.multiple_of(p * YR, YR), YR), :] = step(field1, a, p + 1, p + 1)

    for a in range(3):
        diffuse(a)

    for _, got in fourth:
        got.wait_recv()
    for group in (second, third, fourth):
        for go, _ in group:
            go.wait_send()
    for h in (warp_halo, *field_halo):
        halo_sent(h)
    stif_near.wait_send()

    @pl.when(linked)
    def _():
        stif_far.wait_send()
        for go, _ in shared:
            go.wait_send()


def store(template, velocity, tout, vout, sem):
    one = pltpu.make_async_copy(velocity, vout, sem.at[0])
    two = pltpu.make_async_copy(template, tout, sem.at[1])
    one.start()
    two.start()
    one.wait()
    two.wait()


def per_device(subjects, slabs, template, images, velocity, stiffness, send_rows, ref_slot, columns, weights):
    rows, width = template.shape
    cap = send_rows.shape[3]
    slots = slabs * cap
    planes = rows // YR
    hbm_space = pl.BlockSpec(memory_space=pltpu.HBM)
    dma = pltpu.SemaphoreType.DMA
    vm = pltpu.VMEM
    scratch = [
        vm((rows, width), F32),
        vm((1, rows, width), F32),
        vm((1, 3, rows, width), F32),
        vm((1, 1, slabs, cap), jnp.int32),
        vm((1, NB, rows), jnp.int32),
        vm((rows * NB, width), jnp.int32),
        vm((rows * NB, width), BF),
        vm((rows * NB, width), F32),
        vm((NB, rows, width), jnp.int32),
        vm((NB, rows, width), F32),
        vm((NB, len(OFFSETS), rows, width), F32),
        vm((NB, rows, slots), BF),
        vm((slots, NB * rows), BF),
        vm((slots, rows), BF),
        vm((rows, slots), BF),
        vm((slots, width), F32),
        vm((slots, width), F32),
        vm((slots, 2 * width), BF),
        vm((rows + 2 * YR, width), F32),
        vm((len(OFFSETS), rows, width), F32),
        vm((NB * rows, 2 * width), BF),
        vm((slots, width), F32),
        vm((rows, width), F32),
        vm((rows, width), F32),
        vm((7, rows + 2 * YR, width), F32),
        vm((rows + 4 * YR, width), F32),
        vm((3, rows + 4 * YR, width), F32),
        vm((3, rows + 2 * YR, width), F32),
        dma((8,)),
        dma((slabs,)), dma((slabs,)), dma((slabs,)), dma((slabs,)),
        dma((subjects,)), dma((subjects,)), dma((subjects,)), dma((subjects,)),
        dma((subjects,)), dma((subjects,)), dma((10,)), dma((10,)),
    ]
    outs = (
        jax.ShapeDtypeStruct((rows, width), F32),
        jax.ShapeDtypeStruct((1, 3, rows, width), F32),
    )
    vmem_space = pl.BlockSpec(memory_space=vm)
    new = pl.pallas_call(
        functools.partial(kernel, subjects, slabs, cap),
        out_shape=tuple(vm(o.shape, o.dtype) for o in outs),
        in_specs=[hbm_space] * 8,
        out_specs=(vmem_space, vmem_space),
        scratch_shapes=scratch,
        compiler_params=pltpu.CompilerParams(
            collective_id=0, has_side_effects=True, vmem_limit_bytes=62 * 2**20
        ),
    )(
        template, images, velocity, stiffness, send_rows,
        jnp.transpose(ref_slot, (0, 2, 1)),
        columns.reshape(rows * NB, width),
        weights.reshape(rows * NB, width),
    )
    return pl.pallas_call(
        store,
        out_shape=outs,
        in_specs=[pl.BlockSpec(memory_space=pl.ANY)] * 2,
        out_specs=(hbm_space, hbm_space),
        scratch_shapes=[dma((2,))],
        compiler_params=pltpu.CompilerParams(vmem_limit_bytes=2**20),
    )(*new)


def solution(mesh):
    return jax.shard_map(
        functools.partial(per_device, mesh.shape["subj"], mesh.shape["slab"]),
        mesh=mesh,
        in_specs=(
            P("slab", None),
            P("subj", "slab", None),
            P("subj", None, "slab", None),
            P("slab", None),
            P("subj", "slab", None, None),
            P("subj", "slab", None),
            P("subj", "slab", None, None),
            P("subj", "slab", None, None),
        ),
        out_specs=(P("slab", None), P("subj", None, "slab", None)),
        check_vma=False,
    )
```

```python
import functools
import math

import jax
import jax.numpy as jnp
from jax import lax
from jax.experimental import pallas as pl
from jax.experimental.pallas import tpu as pltpu
from jax.sharding import PartitionSpec as P

YR = 256
NB = 8
HALF_DT = 0.5 * 0.16
FORCE = 1.0
RATE = 2.0
OFFSETS = (-2, -1, 0, 1, 2)
BF = jnp.bfloat16
F32 = jnp.float32


def halves(x):
    hi = x.astype(BF)
    lo = (x - hi.astype(F32)).astype(BF)
    return hi, lo


def torus(outer, inner):
    hops = lambda d, n: min(d, n - d)
    every = [(a, b) for a in range(outer) for b in range(inner) if (a, b) != (0, 0)]
    return sorted(every, key=lambda o: -hops(o[0], outer) - hops(o[1], inner))


def others(me, outer, inner):
    a0, b0 = me // inner, lax.rem(me, inner)
    wrap = lambda at, d, n: jnp.where(at >= n - d, at + d - n, at + d) if d else at
    return [wrap(a0, a, outer) * inner + wrap(b0, b, inner) for a, b in torus(outer, inner)]


def kernel(
    subjects, slabs, cap,
    tmpl, img, vel, stiff, send, slot_t, cols, wts,
    tout, vout,
    tmpl_v, img_v, vel_v, send_v, slot_v, cols_v, wts_v, w32, wd, oh, oht, os, ost,
    outbox, inbox, t2, warp, mis, place, retbox, rowg, subbox, coef, stif, field, field1,
    load_sem, a_send, a_recv, b_send, b_recv, c_send, c_recv, d_send, d_recv, e_send, e_recv, h_send, h_recv,
):
    rows, width = tmpl_v.shape
    slots = slabs * cap
    part = rows // subjects
    me_s = lax.axis_index("subj")
    me_k = lax.axis_index("slab")

    pairs = (
        (send, send_v), (tmpl, tmpl_v), (slot_t, slot_v), (cols, cols_v), (wts, wts_v),
        (stiff, stif.at[pl.ds(2 * YR, rows), :]), (img, img_v), (vel, vel_v),
    )
    loads = [pltpu.make_async_copy(a, b, load_sem.at[i]) for i, (a, b) in enumerate(pairs)]
    for load in loads[:2]:
        load.start()

    side = math.isqrt(subjects)
    rest = {"slab": others(me_k, slabs // 2, 2), "subj": others(me_s, subjects // side, side)}
    barrier = pltpu.get_barrier_semaphore()
    for pair in zip(rest["slab"], rest["subj"]):
        for axis, to in zip(("slab", "subj"), pair):
            pl.semaphore_signal(barrier, inc=1, device_id={axis: to})
    for load in loads[2:]:
        load.start()

    def peers(axis, src, dst, send_sem, recv_sem):
        return [
            pltpu.make_async_remote_copy(
                src_ref=src(to), dst_ref=dst(i), send_sem=send_sem.at[i], recv_sem=recv_sem.at[i], device_id={axis: to},
            )
            for i, to in enumerate(rest[axis])
        ]

    def start(copies):
        for copy in copies:
            copy.start()

    def got(copies):
        for copy in copies:
            copy.wait_recv()

    def sent(copies):
        for copy in copies:
            copy.wait_send()

    loads[0].wait()
    send_c = jnp.transpose(send_v[0, 0])
    lane_r = lax.broadcasted_iota(jnp.int32, (cap, rows), 1)
    for j in range(slabs):
        os[pl.ds(j * cap, cap), :] = jnp.where(send_c[:, j : j + 1] == lane_r, 1.0, 0.0).astype(BF)
    loads[1].wait()
    hi, lo = halves(tmpl_v[...])
    both = jnp.dot(os[...], jnp.concatenate([hi, lo], axis=1), preferred_element_type=F32)
    outbox[...] = both[:, :width] + both[:, width:]

    odd = lax.rem(me_k, 2)
    other = me_k + 1 - 2 * odd
    across = me_k - 1 + 2 * odd
    linked = jnp.logical_and(across >= 0, across < slabs)
    mine = pl.ds(pl.multiple_of(me_s * part, part), part)
    low_at, own_at, high_at = 0, 2 * YR, 2 * YR + rows
    far_in = low_at + odd * (high_at - low_at)
    far_out = high_at - odd * (high_at - low_at)
    stif_near = pltpu.make_async_remote_copy(
        src_ref=stif.at[pl.ds(own_at, rows), :], dst_ref=stif.at[pl.ds(pl.multiple_of(far_in, rows), rows), :],
        send_sem=h_send.at[2], recv_sem=h_recv.at[2], device_id={"slab": other},
    )

    def stif_rows(start):
        return stif.at[pl.ds(pl.multiple_of(start, part), part), :]

    stif_far = pltpu.make_async_remote_copy(
        src_ref=stif_rows(own_at + me_s * part), dst_ref=stif_rows(far_out + me_s * part),
        send_sem=h_send.at[3], recv_sem=h_recv.at[3], device_id={"slab": jnp.clip(across, 0, slabs - 1)},
    )
    loads[5].wait()

    pl.semaphore_wait(barrier, slabs - 1 + subjects - 1)
    pl.when(linked)(stif_far.start)
    own = pl.ds(pl.multiple_of(me_k * cap, cap), cap)
    to_slab = lambda j: outbox.at[pl.ds(pl.multiple_of(j * cap, cap), cap), :]
    first = peers("slab", to_slab, lambda i: inbox.at[own, :], a_send, a_recv)
    start(first)
    inbox[own, :] = outbox[own, :]

    stif_near.start()

    loads[2].wait()
    slot_c = jnp.transpose(slot_v[0])
    lane_q = lax.broadcasted_iota(jnp.int32, (rows, slots), 1)
    sub_q = lax.broadcasted_iota(jnp.int32, (slots, width), 0)
    for b in range(NB):
        oh[b] = jnp.where(slot_c[:, b : b + 1] == lane_q, 1.0, 0.0).astype(BF)
        for c in range(rows // width):
            slot = slot_v[0, b : b + 1, c * width : (c + 1) * width]
            oht[:, pl.ds((c * NB + b) * width, width)] = jnp.where(sub_q == slot, 1.0, 0.0).astype(BF)
    ost[...] = jnp.transpose(os[...].astype(F32)).astype(BF)
    loads[3].wait()
    loads[4].wait()
    w32[...] = wts_v[...].astype(F32)
    lane = lax.broadcasted_iota(jnp.int32, (rows, width), 1)
    for b in range(NB):
        col = cols_v[pl.ds(b, rows, stride=NB), :]
        wgt = w32[pl.ds(b, rows, stride=NB), :]
        off = col - lane
        for n, d in enumerate(OFFSETS):
            kept = jnp.where(off == d, wgt, 0.0)
            wd[b, n] = pltpu.roll(kept, d % width, 1) if d else kept

    low = lax.rem(me_k + slabs - 1, slabs)
    high = lax.rem(me_k + 1, slabs)

    def halo(ref, lead, depth, i):
        inner = rows
        at = lambda start: ref.at[lead + (pl.ds(start, depth), slice(None))]
        base = depth
        down = pltpu.make_async_remote_copy(
            src_ref=at(base), dst_ref=at(base + inner), send_sem=h_send.at[i], recv_sem=h_recv.at[i],
            device_id={"slab": low},
        )
        up = pltpu.make_async_remote_copy(
            src_ref=at(base + inner - depth), dst_ref=at(0), send_sem=h_send.at[i + 1], recv_sem=h_recv.at[i + 1],
            device_id={"slab": high},
        )
        return down, up

    def halo_start(h):
        pl.when(me_k > 0)(h[0].start)
        pl.when(me_k < slabs - 1)(h[1].start)

    def halo_got(h):
        pl.when(me_k < slabs - 1)(h[0].wait_recv)
        pl.when(me_k > 0)(h[1].wait_recv)

    def halo_sent(h):
        pl.when(me_k > 0)(h[0].wait_send)
        pl.when(me_k < slabs - 1)(h[1].wait_send)

    @pl.when(me_k == 0)
    def _():
        warp[pl.ds(0, YR), :] = jnp.zeros((YR, width), F32)
        stif[pl.ds(0, 2 * YR), :] = jnp.zeros((2 * YR, width), F32)
        field[:, pl.ds(0, 2 * YR), :] = jnp.zeros((3, 2 * YR, width), F32)

    @pl.when(me_k == slabs - 1)
    def _():
        warp[pl.ds(YR + rows, YR), :] = jnp.zeros((YR, width), F32)
        stif[pl.ds(2 * YR + rows, 2 * YR), :] = jnp.zeros((2 * YR, width), F32)
        field[:, pl.ds(2 * YR + rows, 2 * YR), :] = jnp.zeros((3, 2 * YR, width), F32)

    warp_halo = halo(warp, (), YR, 0)
    field_halo = [halo(field, (a,), 2 * YR, 4 + 2 * a) for a in range(3)]

    shared = peers(
        "subj",
        lambda s: stif_rows(far_in + me_s * part), lambda i: stif_rows(far_in + me_s * part), e_send, e_recv,
    )

    @pl.when(linked)
    def _():
        stif_far.wait_recv()
        start(shared)

    got(first)
    hi, lo = halves(inbox[...])
    t2[:, :width] = hi
    t2[:, width:] = lo
    loads[6].wait()
    for c in range(rows // width):
        here = pl.ds(c * width, width)
        sums = [None] * len(OFFSETS)
        for b in range(NB):
            both = jnp.dot(oh[b, here, :], t2[...], preferred_element_type=F32)
            picked = both[:, :width] + both[:, width:]
            for n in range(len(OFFSETS)):
                term = wd[b, n, here, :] * picked
                sums[n] = term if sums[n] is None else sums[n] + term
        total = sums[OFFSETS.index(0)]
        for n, d in enumerate(OFFSETS):
            if d:
                total = total + pltpu.roll(sums[n], -d % width, 1)
        warp[pl.ds(YR + c * width, width), :] = total
        apart = total - img_v[0, here, :]
        for n, d in enumerate(OFFSETS):
            mis[n, here, :] = pltpu.roll(apart, d % width, 1) if d else apart
        if (c + 1) * width == YR:
            pl.when(me_k > 0)(warp_halo[0].start)
    pl.when(me_k < slabs - 1)(warp_halo[1].start)

    block = 16
    for c in range(rows // width):
        for q in range(width // block):
            here = pl.ds(c * width + q * block, block)
            apart = [mis[n, here, :] for n in range(len(OFFSETS))]
            for b in range(NB):
                total = wd[b, 0, here, :] * apart[0]
                for n in range(1, len(OFFSETS)):
                    total = total + wd[b, n, here, :] * apart[n]
                hi, lo = halves(total)
                there = pl.ds((c * NB + b) * width + q * block, block)
                place[there, :width] = hi
                place[there, width:] = lo

    sent(first)
    second = peers("slab", to_slab, lambda i: retbox.at[own, :], b_send, b_recv)
    for part_of in range(2):
        here = pl.ds(part_of * (slots // 2), slots // 2)
        both = jnp.dot(oht[here, :], place[...], preferred_element_type=F32)
        outbox[here, :] = both[:, :width] + both[:, width:]
        for copy, to in zip(second, rest["slab"]):
            pl.when((to >= slabs // 2) == bool(part_of))(copy.start)
    retbox[own, :] = outbox[own, :]

    halo_got(warp_halo)
    loads[7].wait()
    lane_p = lax.broadcasted_iota(jnp.int32, (YR, width), 1)
    row_p = lax.broadcasted_iota(jnp.int32, (YR, width), 0)

    def shifted(x):
        left = jnp.where(lane_p == 0, 0.0, pltpu.roll(x, 1, 1))
        right = jnp.where(lane_p == width - 1, 0.0, pltpu.roll(x, width - 1, 1))
        above = jnp.where(row_p == 0, 0.0, pltpu.roll(x, 1, 0))
        below = jnp.where(row_p == YR - 1, 0.0, pltpu.roll(x, YR - 1, 0))
        return left, right, above, below

    def along(x, dim):
        left, right, above, below = shifted(x)
        return right - left if dim else below - above

    for a in range(3):

        @pl.loop(0, rows // YR)
        def _(p):
            plane = lambda i: pl.ds(pl.multiple_of((p + i) * YR, YR), YR)
            if a == 2:
                slope = warp[plane(2), :] - warp[plane(0), :]
            else:
                slope = along(warp[plane(1), :], 1 - a)
            field[a, plane(2), :] = vel_v[0, a, plane(0), :] - (0.5 * FORCE) * mis[2, plane(0), :] * slope

        halo_start(field_halo[a])

    stif_near.wait_recv()

    @pl.when(linked)
    def _():
        got(shared)

    @pl.loop(0, rows // YR + 2)
    def _(p):
        plane = me_k * (rows // YR) + p
        inside = jnp.where(jnp.logical_and(plane >= 1, plane <= slabs * (rows // YR)), 1.0, 0.0)
        here = pl.ds(pl.multiple_of(p * YR, YR), YR)
        centre = stif[pl.ds(pl.multiple_of((p + 1) * YR, YR), YR), :]
        before = stif[here, :]
        after = stif[pl.ds(pl.multiple_of((p + 2) * YR, YR), YR), :]
        near = shifted(centre)
        scale = inside * HALF_DT
        edges = (lane_p == 0, lane_p == width - 1, row_p == 0, row_p == YR - 1)
        spent = 6.0 * centre + before + after
        for n in range(4):
            coef[n, here, :] = jnp.where(edges[n], 0.0, scale * (centre + near[n]))
            spent = spent + near[n]
        coef[4, here, :] = scale * (centre + before)
        coef[5, here, :] = scale * (centre + after)
        coef[6, here, :] = inside - scale * spent

    got(second)
    hi, lo = halves(retbox[...])
    back = jnp.concatenate([hi, lo], axis=1)
    third = peers(
        "subj", lambda s: rowg.at[pl.ds(pl.multiple_of(s * part, part), part), :], lambda i: subbox.at[i], c_send, c_recv,
    )
    for part_of in range(2):
        here = pl.ds(part_of * (rows // 2), rows // 2)
        both = jnp.dot(ost[here, :], back, preferred_element_type=F32)
        rowg[here, :] = both[:, :width] + both[:, width:]
        for copy, to in zip(third, rest["subj"]):
            pl.when((to >= subjects // 2) == bool(part_of))(copy.start)
    total = rowg[mine, :]
    got(third)
    for i in range(subjects - 1):
        total = total + subbox[i]
    tout[mine, :] = tmpl_v[mine, :] - (RATE / subjects) * total
    fourth = peers("subj", lambda s: tout.at[mine, :], lambda i: tout.at[mine, :], d_send, d_recv)
    start(fourth)

    def step(src, lead, p, q):
        at = lambda i: pl.ds(pl.multiple_of(i * YR, YR), YR)
        x = src[lead, at(p), :]
        c = lambda n: coef[n, at(q), :]
        out = c(6) * x
        out = out + c(0) * pltpu.roll(x, 1, 1)
        out = out + c(1) * pltpu.roll(x, width - 1, 1)
        out = out + c(2) * pltpu.roll(x, 1, 0)
        out = out + c(3) * pltpu.roll(x, YR - 1, 0)
        out = out + c(4) * src[lead, at(p - 1), :]
        return out + c(5) * src[lead, at(p + 1), :]

    def diffuse(a):
        halo_got(field_halo[a])

        @pl.loop(0, rows // YR + 2)
        def _(p):
            field1[a, pl.ds(pl.multiple_of(p * YR, YR), YR), :] = step(field, a, p + 1, p)

        @pl.loop(0, rows // YR)
        def _(p):
            vout[0, a, pl.ds(pl.multiple_of(p * YR, YR), YR), :] = step(field1, a, p + 1, p + 1)

    for a in range(3):
        diffuse(a)

    for group in (second, third):
        sent(group)
    for h in (warp_halo, *field_halo):
        halo_sent(h)
    stif_near.wait_send()

    @pl.when(linked)
    def _():
        stif_far.wait_send()
        sent(shared)

    got(fourth)
    sent(fourth)


def store(template, velocity, tout, vout, sem):
    one = pltpu.make_async_copy(velocity, vout, sem.at[0])
    two = pltpu.make_async_copy(template, tout, sem.at[1])
    one.start()
    two.start()
    one.wait()
    two.wait()


def per_device(subjects, slabs, template, images, velocity, stiffness, send_rows, ref_slot, columns, weights):
    rows, width = template.shape
    cap = send_rows.shape[3]
    slots = slabs * cap
    planes = rows // YR
    hbm_space = pl.BlockSpec(memory_space=pltpu.HBM)
    dma = pltpu.SemaphoreType.DMA
    vm = pltpu.VMEM
    scratch = [
        vm((rows, width), F32),
        vm((1, rows, width), F32),
        vm((1, 3, rows, width), F32),
        vm((1, 1, slabs, cap), jnp.int32),
        vm((1, NB, rows), jnp.int32),
        vm((rows * NB, width), jnp.int32),
        vm((rows * NB, width), BF),
        vm((rows * NB, width), F32),
        vm((NB, len(OFFSETS), rows, width), F32),
        vm((NB, rows, slots), BF),
        vm((slots, NB * rows), BF),
        vm((slots, rows), BF),
        vm((rows, slots), BF),
        vm((slots, width), F32),
        vm((slots, width), F32),
        vm((slots, 2 * width), BF),
        vm((rows + 2 * YR, width), F32),
        vm((len(OFFSETS), rows, width), F32),
        vm((NB * rows, 2 * width), BF),
        vm((slots, width), F32),
        vm((rows, width), F32),
        vm((subjects - 1, rows // subjects, width), F32),
        vm((7, rows + 2 * YR, width), F32),
        vm((rows + 4 * YR, width), F32),
        vm((3, rows + 4 * YR, width), F32),
        vm((3, rows + 2 * YR, width), F32),
        dma((8,)),
        dma((slabs,)), dma((slabs,)), dma((slabs,)), dma((slabs,)),
        dma((subjects,)), dma((subjects,)), dma((subjects,)), dma((subjects,)),
        dma((subjects,)), dma((subjects,)), dma((10,)), dma((10,)),
    ]
    outs = (
        jax.ShapeDtypeStruct((rows, width), F32),
        jax.ShapeDtypeStruct((1, 3, rows, width), F32),
    )
    vmem_space = pl.BlockSpec(memory_space=vm)
    new = pl.pallas_call(
        functools.partial(kernel, subjects, slabs, cap),
        out_shape=tuple(vm(o.shape, o.dtype) for o in outs),
        in_specs=[hbm_space] * 8,
        out_specs=(vmem_space, vmem_space),
        scratch_shapes=scratch,
        compiler_params=pltpu.CompilerParams(
            collective_id=0, has_side_effects=True, vmem_limit_bytes=62 * 2**20
        ),
    )(
        template, images, velocity, stiffness, send_rows,
        jnp.transpose(ref_slot, (0, 2, 1)),
        columns.reshape(rows * NB, width),
        weights.reshape(rows * NB, width),
    )
    return pl.pallas_call(
        store,
        out_shape=outs,
        in_specs=[pl.BlockSpec(memory_space=pl.ANY)] * 2,
        out_specs=(hbm_space, hbm_space),
        scratch_shapes=[dma((2,))],
        compiler_params=pltpu.CompilerParams(vmem_limit_bytes=2**20),
    )(*new)


def solution(mesh):
    return jax.shard_map(
        functools.partial(per_device, mesh.shape["subj"], mesh.shape["slab"]),
        mesh=mesh,
        in_specs=(
            P("slab", None),
            P("subj", "slab", None),
            P("subj", None, "slab", None),
            P("slab", None),
            P("subj", "slab", None, None),
            P("subj", "slab", None),
            P("subj", "slab", None, None),
            P("subj", "slab", None, None),
        ),
        out_specs=(P("slab", None), P("subj", None, "slab", None)),
        check_vma=False,
    )
```

```python
import functools
import math

import jax
import jax.numpy as jnp
from jax import lax
from jax.experimental import pallas as pl
from jax.experimental.pallas import tpu as pltpu
from jax.sharding import PartitionSpec as P

YR = 256
NB = 8
HALF_DT = 0.5 * 0.16
FORCE = 1.0
RATE = 2.0
OFFSETS = (-2, -1, 0, 1, 2)
BF = jnp.bfloat16
F32 = jnp.float32


def halves(x):
    hi = x.astype(BF)
    lo = (x - hi.astype(F32)).astype(BF)
    return hi, lo


def torus(outer, inner):
    hops = lambda d, n: min(d, n - d)
    every = [(a, b) for a in range(outer) for b in range(inner) if (a, b) != (0, 0)]
    return sorted(every, key=lambda o: -hops(o[0], outer) - hops(o[1], inner))


def others(me, outer, inner):
    a0, b0 = me // inner, lax.rem(me, inner)
    wrap = lambda at, d, n: jnp.where(at >= n - d, at + d - n, at + d) if d else at
    return [wrap(a0, a, outer) * inner + wrap(b0, b, inner) for a, b in torus(outer, inner)]


def kernel(
    subjects, slabs, cap,
    tmpl, img, vel, stiff, send, slot_t, cols, wts,
    tout, vout,
    tmpl_v, img_v, vel_v, send_v, slot_v, cols_v, wts_v, w32, wd, oh, oht, os, ost, slot_id, row_id,
    outbox, inbox, t2, warp, mis, place, retbox, rowg, subbox, coef, stif, field, field1,
    load_sem, a_send, a_recv, b_send, b_recv, c_send, c_recv, d_send, d_recv, e_send, e_recv, h_send, h_recv,
):
    rows, width = tmpl_v.shape
    slots = slabs * cap
    part = rows // subjects
    me_s = lax.axis_index("subj")
    me_k = lax.axis_index("slab")

    pairs = (
        (send, send_v), (tmpl, tmpl_v), (slot_t, slot_v), (cols, cols_v), (wts, wts_v),
        (stiff, stif.at[pl.ds(2 * YR, rows), :]), (img, img_v), (vel, vel_v),
    )
    loads = [pltpu.make_async_copy(a, b, load_sem.at[i]) for i, (a, b) in enumerate(pairs)]
    for load in loads[:2]:
        load.start()

    side = math.isqrt(subjects)
    rest = {"slab": others(me_k, slabs // 2, 2), "subj": others(me_s, subjects // side, side)}
    barrier = pltpu.get_barrier_semaphore()
    for pair in zip(rest["slab"], rest["subj"]):
        for axis, to in zip(("slab", "subj"), pair):
            pl.semaphore_signal(barrier, inc=1, device_id={axis: to})
    for load in loads[2:]:
        load.start()

    def peers(axis, src, dst, send_sem, recv_sem):
        return [
            pltpu.make_async_remote_copy(
                src_ref=src(i, to), dst_ref=dst(i), send_sem=send_sem.at[i], recv_sem=recv_sem.at[i], device_id={axis: to},
            )
            for i, to in enumerate(rest[axis])
        ]

    def start(copies):
        for copy in copies:
            copy.start()

    def got(copies):
        for copy in copies:
            copy.wait_recv()

    def sent(copies):
        for copy in copies:
            copy.wait_send()

    loads[0].wait()
    send_c = jnp.transpose(send_v[0, 0])
    lane_r = lax.broadcasted_iota(jnp.int32, (cap, rows), 1)
    for j in range(slabs):
        os[pl.ds(j * cap, cap), :] = jnp.where(send_c[:, j : j + 1] == lane_r, 1.0, 0.0).astype(BF)
    loads[1].wait()
    hi, lo = halves(tmpl_v[...])
    both = jnp.dot(os[...], jnp.concatenate([hi, lo], axis=1), preferred_element_type=F32)
    outbox[...] = both[:, :width] + both[:, width:]

    odd = lax.rem(me_k, 2)
    other = me_k + 1 - 2 * odd
    across = me_k - 1 + 2 * odd
    linked = jnp.logical_and(across >= 0, across < slabs)
    mine = pl.ds(pl.multiple_of(me_s * part, part), part)
    low_at, own_at, high_at = 0, 2 * YR, 2 * YR + rows
    far_in = low_at + odd * (high_at - low_at)
    far_out = high_at - odd * (high_at - low_at)
    stif_near = pltpu.make_async_remote_copy(
        src_ref=stif.at[pl.ds(own_at, rows), :], dst_ref=stif.at[pl.ds(pl.multiple_of(far_in, rows), rows), :],
        send_sem=h_send.at[2], recv_sem=h_recv.at[2], device_id={"slab": other},
    )

    def stif_rows(start):
        return stif.at[pl.ds(pl.multiple_of(start, part), part), :]

    stif_far = pltpu.make_async_remote_copy(
        src_ref=stif_rows(own_at + me_s * part), dst_ref=stif_rows(far_out + me_s * part),
        send_sem=h_send.at[3], recv_sem=h_recv.at[3], device_id={"slab": jnp.clip(across, 0, slabs - 1)},
    )
    pl.semaphore_wait(barrier, slabs - 1 + subjects - 1)
    own = pl.ds(pl.multiple_of(me_k * cap, cap), cap)
    to_slab = lambda i, j: outbox.at[pl.ds(pl.multiple_of(j * cap, cap), cap), :]
    first = peers("slab", to_slab, lambda i: inbox.at[own, :], a_send, a_recv)
    start(first)
    inbox[own, :] = outbox[own, :]

    loads[5].wait()
    pl.when(linked)(stif_far.start)
    stif_near.start()

    loads[2].wait()
    slot_c = jnp.transpose(slot_v[0])
    lane_q = lax.broadcasted_iota(jnp.int32, (rows, slots), 1)
    for i, to in enumerate([*rest["slab"], me_k]):
        slot_id[pl.ds(i * cap, cap), :] = lax.broadcasted_iota(jnp.int32, (cap, width), 0) + to * cap
    for i, to in enumerate([*rest["subj"], me_s]):
        row_id[pl.ds(i * part, part), :] = lax.broadcasted_iota(jnp.int32, (part, width), 0) + to * part
    for b in range(NB):
        oh[b] = jnp.where(slot_c[:, b : b + 1] == lane_q, 1.0, 0.0).astype(BF)
        for c in range(rows // width):
            slot = slot_v[0, b : b + 1, c * width : (c + 1) * width]
            oht[:, pl.ds((c * NB + b) * width, width)] = jnp.where(slot_id[...] == slot, 1.0, 0.0).astype(BF)
    for t in range(slots // width):
        held = [jnp.broadcast_to(send_c[:, j : j + 1], (cap, width)) for j in range(t * width // cap, (t + 1) * width // cap)]
        row = jnp.transpose(jnp.concatenate(held, axis=0))[:1, :]
        ost[:, pl.ds(t * width, width)] = jnp.where(row_id[...] == row, 1.0, 0.0).astype(BF)
    loads[3].wait()
    loads[4].wait()
    w32[...] = wts_v[...].astype(F32)
    lane = lax.broadcasted_iota(jnp.int32, (rows, width), 1)
    for b in range(NB):
        col = cols_v[pl.ds(b, rows, stride=NB), :]
        wgt = w32[pl.ds(b, rows, stride=NB), :]
        off = col - lane
        for n, d in enumerate(OFFSETS):
            kept = jnp.where(off == d, wgt, 0.0)
            wd[b, n] = pltpu.roll(kept, d % width, 1) if d else kept

    low = lax.rem(me_k + slabs - 1, slabs)
    high = lax.rem(me_k + 1, slabs)

    def halo(ref, lead, depth, i):
        inner = rows
        at = lambda start: ref.at[lead + (pl.ds(start, depth), slice(None))]
        base = depth
        down = pltpu.make_async_remote_copy(
            src_ref=at(base), dst_ref=at(base + inner), send_sem=h_send.at[i], recv_sem=h_recv.at[i],
            device_id={"slab": low},
        )
        up = pltpu.make_async_remote_copy(
            src_ref=at(base + inner - depth), dst_ref=at(0), send_sem=h_send.at[i + 1], recv_sem=h_recv.at[i + 1],
            device_id={"slab": high},
        )
        return down, up

    def halo_start(h):
        pl.when(me_k > 0)(h[0].start)
        pl.when(me_k < slabs - 1)(h[1].start)

    def halo_got(h):
        pl.when(me_k < slabs - 1)(h[0].wait_recv)
        pl.when(me_k > 0)(h[1].wait_recv)

    def halo_sent(h):
        pl.when(me_k > 0)(h[0].wait_send)
        pl.when(me_k < slabs - 1)(h[1].wait_send)

    @pl.when(me_k == 0)
    def _():
        warp[pl.ds(0, YR), :] = jnp.zeros((YR, width), F32)
        stif[pl.ds(0, 2 * YR), :] = jnp.zeros((2 * YR, width), F32)
        field[:, pl.ds(0, 2 * YR), :] = jnp.zeros((3, 2 * YR, width), F32)

    @pl.when(me_k == slabs - 1)
    def _():
        warp[pl.ds(YR + rows, YR), :] = jnp.zeros((YR, width), F32)
        stif[pl.ds(2 * YR + rows, 2 * YR), :] = jnp.zeros((2 * YR, width), F32)
        field[:, pl.ds(2 * YR + rows, 2 * YR), :] = jnp.zeros((3, 2 * YR, width), F32)

    warp_halo = halo(warp, (), YR, 0)
    field_halo = [halo(field, (a,), 2 * YR, 4 + 2 * a) for a in range(3)]

    shared = peers(
        "subj",
        lambda i, s: stif_rows(far_in + me_s * part), lambda i: stif_rows(far_in + me_s * part), e_send, e_recv,
    )

    @pl.when(linked)
    def _():
        stif_far.wait_recv()
        start(shared)

    got(first)
    hi, lo = halves(inbox[...])
    t2[:, :width] = hi
    t2[:, width:] = lo
    loads[6].wait()
    for c in range(rows // width):
        here = pl.ds(c * width, width)
        sums = [None] * len(OFFSETS)
        for b in range(NB):
            both = jnp.dot(oh[b, here, :], t2[...], preferred_element_type=F32)
            picked = both[:, :width] + both[:, width:]
            for n in range(len(OFFSETS)):
                term = wd[b, n, here, :] * picked
                sums[n] = term if sums[n] is None else sums[n] + term
        total = sums[OFFSETS.index(0)]
        for n, d in enumerate(OFFSETS):
            if d:
                total = total + pltpu.roll(sums[n], -d % width, 1)
        warp[pl.ds(YR + c * width, width), :] = total
        apart = total - img_v[0, here, :]
        for n, d in enumerate(OFFSETS):
            mis[n, here, :] = pltpu.roll(apart, d % width, 1) if d else apart
        if (c + 1) * width == YR:
            pl.when(me_k > 0)(warp_halo[0].start)
    pl.when(me_k < slabs - 1)(warp_halo[1].start)

    block = 16
    for c in range(rows // width):
        for q in range(width // block):
            here = pl.ds(c * width + q * block, block)
            apart = [mis[n, here, :] for n in range(len(OFFSETS))]
            for b in range(NB):
                total = wd[b, 0, here, :] * apart[0]
                for n in range(1, len(OFFSETS)):
                    total = total + wd[b, n, here, :] * apart[n]
                hi, lo = halves(total)
                there = pl.ds((c * NB + b) * width + q * block, block)
                place[there, :width] = hi
                place[there, width:] = lo

    sent(first)
    second = peers("slab", lambda i, j: outbox.at[pl.ds(i * cap, cap), :], lambda i: retbox.at[own, :], b_send, b_recv)
    for part_of in range(2):
        here = pl.ds(part_of * (slots // 2), slots // 2)
        both = jnp.dot(oht[here, :], place[...], preferred_element_type=F32)
        outbox[here, :] = both[:, :width] + both[:, width:]
        start(second[part_of * slabs // 2 : (part_of + 1) * slabs // 2])
    retbox[own, :] = outbox[pl.ds(slots - cap, cap), :]

    halo_got(warp_halo)
    loads[7].wait()
    lane_p = lax.broadcasted_iota(jnp.int32, (YR, width), 1)
    row_p = lax.broadcasted_iota(jnp.int32, (YR, width), 0)

    def shifted(x):
        left = jnp.where(lane_p == 0, 0.0, pltpu.roll(x, 1, 1))
        right = jnp.where(lane_p == width - 1, 0.0, pltpu.roll(x, width - 1, 1))
        above = jnp.where(row_p == 0, 0.0, pltpu.roll(x, 1, 0))
        below = jnp.where(row_p == YR - 1, 0.0, pltpu.roll(x, YR - 1, 0))
        return left, right, above, below

    def along(x, dim):
        left, right, above, below = shifted(x)
        return right - left if dim else below - above

    for a in range(3):

        @pl.loop(0, rows // YR)
        def _(p):
            plane = lambda i: pl.ds(pl.multiple_of((p + i) * YR, YR), YR)
            if a == 2:
                slope = warp[plane(2), :] - warp[plane(0), :]
            else:
                slope = along(warp[plane(1), :], 1 - a)
            field[a, plane(2), :] = vel_v[0, a, plane(0), :] - (0.5 * FORCE) * mis[2, plane(0), :] * slope

        halo_start(field_halo[a])

    stif_near.wait_recv()

    @pl.when(linked)
    def _():
        got(shared)

    @pl.loop(0, rows // YR + 2)
    def _(p):
        plane = me_k * (rows // YR) + p
        inside = jnp.where(jnp.logical_and(plane >= 1, plane <= slabs * (rows // YR)), 1.0, 0.0)
        here = pl.ds(pl.multiple_of(p * YR, YR), YR)
        centre = stif[pl.ds(pl.multiple_of((p + 1) * YR, YR), YR), :]
        before = stif[here, :]
        after = stif[pl.ds(pl.multiple_of((p + 2) * YR, YR), YR), :]
        near = shifted(centre)
        scale = inside * HALF_DT
        edges = (lane_p == 0, lane_p == width - 1, row_p == 0, row_p == YR - 1)
        spent = 6.0 * centre + before + after
        for n in range(4):
            coef[n, here, :] = jnp.where(edges[n], 0.0, scale * (centre + near[n]))
            spent = spent + near[n]
        coef[4, here, :] = scale * (centre + before)
        coef[5, here, :] = scale * (centre + after)
        coef[6, here, :] = inside - scale * spent

    got(second)
    hi, lo = halves(retbox[...])
    back = jnp.concatenate([hi, lo], axis=1)
    third = peers(
        "subj", lambda i, s: rowg.at[pl.ds(i * part, part), :], lambda i: subbox.at[i], c_send, c_recv,
    )
    for part_of in range(2):
        here = pl.ds(part_of * (rows // 2), rows // 2)
        both = jnp.dot(ost[here, :], back, preferred_element_type=F32)
        rowg[here, :] = both[:, :width] + both[:, width:]
        start(third[part_of * subjects // 2 : (part_of + 1) * subjects // 2])
    total = rowg[pl.ds(rows - part, part), :]
    got(third)
    for i in range(subjects - 1):
        total = total + subbox[i]
    tout[mine, :] = tmpl_v[mine, :] - (RATE / subjects) * total
    fourth = peers("subj", lambda i, s: tout.at[mine, :], lambda i: tout.at[mine, :], d_send, d_recv)
    start(fourth)

    def step(src, lead, p, q):
        at = lambda i: pl.ds(pl.multiple_of(i * YR, YR), YR)
        x = src[lead, at(p), :]
        c = lambda n: coef[n, at(q), :]
        out = c(6) * x
        out = out + c(0) * pltpu.roll(x, 1, 1)
        out = out + c(1) * pltpu.roll(x, width - 1, 1)
        out = out + c(2) * pltpu.roll(x, 1, 0)
        out = out + c(3) * pltpu.roll(x, YR - 1, 0)
        out = out + c(4) * src[lead, at(p - 1), :]
        return out + c(5) * src[lead, at(p + 1), :]

    def diffuse(a):
        halo_got(field_halo[a])

        @pl.loop(0, rows // YR + 2)
        def _(p):
            field1[a, pl.ds(pl.multiple_of(p * YR, YR), YR), :] = step(field, a, p + 1, p)

        @pl.loop(0, rows // YR)
        def _(p):
            vout[0, a, pl.ds(pl.multiple_of(p * YR, YR), YR), :] = step(field1, a, p + 1, p + 1)

    for a in range(3):
        diffuse(a)

    for group in (second, third):
        sent(group)
    for h in (warp_halo, *field_halo):
        halo_sent(h)
    stif_near.wait_send()

    @pl.when(linked)
    def _():
        stif_far.wait_send()
        sent(shared)

    got(fourth)
    sent(fourth)


def store(template, velocity, tout, vout, sem):
    one = pltpu.make_async_copy(velocity, vout, sem.at[0])
    two = pltpu.make_async_copy(template, tout, sem.at[1])
    one.start()
    two.start()
    one.wait()
    two.wait()


def per_device(subjects, slabs, template, images, velocity, stiffness, send_rows, ref_slot, columns, weights):
    rows, width = template.shape
    cap = send_rows.shape[3]
    slots = slabs * cap
    planes = rows // YR
    hbm_space = pl.BlockSpec(memory_space=pltpu.HBM)
    dma = pltpu.SemaphoreType.DMA
    vm = pltpu.VMEM
    scratch = [
        vm((rows, width), F32),
        vm((1, rows, width), F32),
        vm((1, 3, rows, width), F32),
        vm((1, 1, slabs, cap), jnp.int32),
        vm((1, NB, rows), jnp.int32),
        vm((rows * NB, width), jnp.int32),
        vm((rows * NB, width), BF),
        vm((rows * NB, width), F32),
        vm((NB, len(OFFSETS), rows, width), F32),
        vm((NB, rows, slots), BF),
        vm((slots, NB * rows), BF),
        vm((slots, rows), BF),
        vm((rows, slots), BF),
        vm((slots, width), jnp.int32),
        vm((rows, width), jnp.int32),
        vm((slots, width), F32),
        vm((slots, width), F32),
        vm((slots, 2 * width), BF),
        vm((rows + 2 * YR, width), F32),
        vm((len(OFFSETS), rows, width), F32),
        vm((NB * rows, 2 * width), BF),
        vm((slots, width), F32),
        vm((rows, width), F32),
        vm((subjects - 1, rows // subjects, width), F32),
        vm((7, rows + 2 * YR, width), F32),
        vm((rows + 4 * YR, width), F32),
        vm((3, rows + 4 * YR, width), F32),
        vm((3, rows + 2 * YR, width), F32),
        dma((8,)),
        dma((slabs,)), dma((slabs,)), dma((slabs,)), dma((slabs,)),
        dma((subjects,)), dma((subjects,)), dma((subjects,)), dma((subjects,)),
        dma((subjects,)), dma((subjects,)), dma((10,)), dma((10,)),
    ]
    outs = (
        jax.ShapeDtypeStruct((rows, width), F32),
        jax.ShapeDtypeStruct((1, 3, rows, width), F32),
    )
    vmem_space = pl.BlockSpec(memory_space=vm)
    new = pl.pallas_call(
        functools.partial(kernel, subjects, slabs, cap),
        out_shape=tuple(vm(o.shape, o.dtype) for o in outs),
        in_specs=[hbm_space] * 8,
        out_specs=(vmem_space, vmem_space),
        scratch_shapes=scratch,
        compiler_params=pltpu.CompilerParams(
            collective_id=0, has_side_effects=True, vmem_limit_bytes=62 * 2**20
        ),
    )(
        template, images, velocity, stiffness, send_rows,
        jnp.transpose(ref_slot, (0, 2, 1)),
        columns.reshape(rows * NB, width),
        weights.reshape(rows * NB, width),
    )
    return pl.pallas_call(
        store,
        out_shape=outs,
        in_specs=[pl.BlockSpec(memory_space=pl.ANY)] * 2,
        out_specs=(hbm_space, hbm_space),
        scratch_shapes=[dma((2,))],
        compiler_params=pltpu.CompilerParams(vmem_limit_bytes=2**20),
    )(*new)


def solution(mesh):
    return jax.shard_map(
        functools.partial(per_device, mesh.shape["subj"], mesh.shape["slab"]),
        mesh=mesh,
        in_specs=(
            P("slab", None),
            P("subj", "slab", None),
            P("subj", None, "slab", None),
            P("slab", None),
            P("subj", "slab", None, None),
            P("subj", "slab", None),
            P("subj", "slab", None, None),
            P("subj", "slab", None, None),
        ),
        out_specs=(P("slab", None), P("subj", None, "slab", None)),
        check_vma=False,
    )
```

```python
import functools
import math

import jax
import jax.numpy as jnp
from jax import lax
from jax.experimental import pallas as pl
from jax.experimental.pallas import tpu as pltpu
from jax.sharding import PartitionSpec as P

YR = 256
NB = 8
HALF_DT = 0.5 * 0.16
FORCE = 1.0
RATE = 2.0
OFFSETS = (-2, -1, 0, 1, 2)
BF = jnp.bfloat16
F32 = jnp.float32


def halves(x):
    hi = x.astype(BF)
    lo = (x - hi.astype(F32)).astype(BF)
    return hi, lo


def torus(outer, inner):
    hops = lambda d, n: min(d, n - d)
    every = [(a, b) for a in range(outer) for b in range(inner) if (a, b) != (0, 0)]
    return sorted(every, key=lambda o: -hops(o[0], outer) - hops(o[1], inner))


def others(me, outer, inner):
    a0, b0 = me // inner, lax.rem(me, inner)
    wrap = lambda at, d, n: jnp.where(at >= n - d, at + d - n, at + d) if d else at
    return [wrap(a0, a, outer) * inner + wrap(b0, b, inner) for a, b in torus(outer, inner)]


def kernel(
    subjects, slabs, cap,
    tmpl, img, vel, stiff, send, slot_t, cols, wts,
    tout, vout,
    tmpl_v, img_v, vel_v, send_v, slot_v, cols_v, wts_v, w32, wd, oh, oht, os, ost,
    outbox, inbox, t2, warp, mis, place, retbox, rowg, subbox, coef, stif, field, field1,
    load_sem, a_send, a_recv, b_send, b_recv, c_send, c_recv, d_send, d_recv, e_send, e_recv, h_send, h_recv,
):
    rows, width = tmpl_v.shape
    slots = slabs * cap
    part = rows // subjects
    me_s = lax.axis_index("subj")
    me_k = lax.axis_index("slab")

    pairs = (
        (send, send_v), (tmpl, tmpl_v), (slot_t, slot_v), (cols, cols_v), (wts, wts_v),
        (stiff, stif.at[pl.ds(2 * YR, rows), :]), (img, img_v), (vel, vel_v),
    )
    loads = [pltpu.make_async_copy(a, b, load_sem.at[i]) for i, (a, b) in enumerate(pairs)]
    for load in loads[:2]:
        load.start()

    side = math.isqrt(subjects)
    rest = {"slab": others(me_k, slabs // 2, 2), "subj": others(me_s, subjects // side, side)}
    barrier = pltpu.get_barrier_semaphore()
    for pair in zip(rest["slab"], rest["subj"]):
        for axis, to in zip(("slab", "subj"), pair):
            pl.semaphore_signal(barrier, inc=1, device_id={axis: to})
    for load in loads[2:]:
        load.start()

    def peers(axis, src, dst, send_sem, recv_sem):
        return [
            pltpu.make_async_remote_copy(
                src_ref=src(to), dst_ref=dst(i), send_sem=send_sem.at[i], recv_sem=recv_sem.at[i], device_id={axis: to},
            )
            for i, to in enumerate(rest[axis])
        ]

    def start(copies):
        for copy in copies:
            copy.start()

    def got(copies):
        for copy in copies:
            copy.wait_recv()

    def sent(copies):
        for copy in copies:
            copy.wait_send()

    loads[0].wait()
    send_c = jnp.transpose(send_v[0, 0])
    lane_r = lax.broadcasted_iota(jnp.int32, (cap, rows), 1)
    for j in range(slabs):
        os[pl.ds(j * cap, cap), :] = jnp.where(send_c[:, j : j + 1] == lane_r, 1.0, 0.0).astype(BF)
    loads[1].wait()
    hi, lo = halves(tmpl_v[...])
    both = jnp.dot(os[...], jnp.concatenate([hi, lo], axis=1), preferred_element_type=F32)
    outbox[...] = both[:, :width] + both[:, width:]

    odd = lax.rem(me_k, 2)
    other = me_k + 1 - 2 * odd
    across = me_k - 1 + 2 * odd
    linked = jnp.logical_and(across >= 0, across < slabs)
    mine = pl.ds(pl.multiple_of(me_s * part, part), part)
    low_at, own_at, high_at = 0, 2 * YR, 2 * YR + rows
    far_in = low_at + odd * (high_at - low_at)
    far_out = high_at - odd * (high_at - low_at)
    stif_near = pltpu.make_async_remote_copy(
        src_ref=stif.at[pl.ds(own_at, rows), :], dst_ref=stif.at[pl.ds(pl.multiple_of(far_in, rows), rows), :],
        send_sem=h_send.at[2], recv_sem=h_recv.at[2], device_id={"slab": other},
    )

    def stif_rows(start):
        return stif.at[pl.ds(pl.multiple_of(start, part), part), :]

    stif_far = pltpu.make_async_remote_copy(
        src_ref=stif_rows(own_at + me_s * part), dst_ref=stif_rows(far_out + me_s * part),
        send_sem=h_send.at[3], recv_sem=h_recv.at[3], device_id={"slab": jnp.clip(across, 0, slabs - 1)},
    )
    loads[5].wait()

    pl.semaphore_wait(barrier, slabs - 1 + subjects - 1)
    pl.when(linked)(stif_far.start)
    own = pl.ds(pl.multiple_of(me_k * cap, cap), cap)
    to_slab = lambda j: outbox.at[pl.ds(pl.multiple_of(j * cap, cap), cap), :]
    first = peers("slab", to_slab, lambda i: inbox.at[own, :], a_send, a_recv)
    start(first)
    inbox[own, :] = outbox[own, :]

    stif_near.start()

    loads[2].wait()
    slot_c = jnp.transpose(slot_v[0])
    lane_q = lax.broadcasted_iota(jnp.int32, (rows, slots), 1)
    sub_q = lax.broadcasted_iota(jnp.int32, (slots, width), 0)
    for b in range(NB):
        oh[b] = jnp.where(slot_c[:, b : b + 1] == lane_q, 1.0, 0.0).astype(BF)
        for c in range(rows // width):
            slot = slot_v[0, b : b + 1, c * width : (c + 1) * width]
            oht[:, pl.ds((c * NB + b) * width, width)] = jnp.where(sub_q == slot, 1.0, 0.0).astype(BF)
    loads[3].wait()
    loads[4].wait()
    w32[...] = wts_v[...].astype(F32)
    lane = lax.broadcasted_iota(jnp.int32, (rows, width), 1)
    for b in range(NB):
        col = cols_v[pl.ds(b, rows, stride=NB), :]
        wgt = w32[pl.ds(b, rows, stride=NB), :]
        off = col - lane
        for n, d in enumerate(OFFSETS):
            kept = jnp.where(off == d, wgt, 0.0)
            wd[b, n] = pltpu.roll(kept, d % width, 1) if d else kept

    low = lax.rem(me_k + slabs - 1, slabs)
    high = lax.rem(me_k + 1, slabs)

    def halo(ref, lead, depth, i):
        inner = rows
        at = lambda start: ref.at[lead + (pl.ds(start, depth), slice(None))]
        base = depth
        down = pltpu.make_async_remote_copy(
            src_ref=at(base), dst_ref=at(base + inner), send_sem=h_send.at[i], recv_sem=h_recv.at[i],
            device_id={"slab": low},
        )
        up = pltpu.make_async_remote_copy(
            src_ref=at(base + inner - depth), dst_ref=at(0), send_sem=h_send.at[i + 1], recv_sem=h_recv.at[i + 1],
            device_id={"slab": high},
        )
        return down, up

    def halo_start(h):
        pl.when(me_k > 0)(h[0].start)
        pl.when(me_k < slabs - 1)(h[1].start)

    def halo_got(h):
        pl.when(me_k < slabs - 1)(h[0].wait_recv)
        pl.when(me_k > 0)(h[1].wait_recv)

    def halo_sent(h):
        pl.when(me_k > 0)(h[0].wait_send)
        pl.when(me_k < slabs - 1)(h[1].wait_send)

    @pl.when(me_k == 0)
    def _():
        warp[pl.ds(0, YR), :] = jnp.zeros((YR, width), F32)
        stif[pl.ds(0, 2 * YR), :] = jnp.zeros((2 * YR, width), F32)
        field[:, pl.ds(0, 2 * YR), :] = jnp.zeros((3, 2 * YR, width), F32)

    @pl.when(me_k == slabs - 1)
    def _():
        warp[pl.ds(YR + rows, YR), :] = jnp.zeros((YR, width), F32)
        stif[pl.ds(2 * YR + rows, 2 * YR), :] = jnp.zeros((2 * YR, width), F32)
        field[:, pl.ds(2 * YR + rows, 2 * YR), :] = jnp.zeros((3, 2 * YR, width), F32)

    warp_halo = halo(warp, (), YR, 0)
    field_halo = [halo(field, (a,), 2 * YR, 4 + 2 * a) for a in range(3)]

    shared = peers(
        "subj",
        lambda s: stif_rows(far_in + me_s * part), lambda i: stif_rows(far_in + me_s * part), e_send, e_recv,
    )

    got(first)
    hi, lo = halves(inbox[...])
    t2[:, :width] = hi
    t2[:, width:] = lo
    loads[6].wait()
    for c in range(rows // width):
        here = pl.ds(c * width, width)
        sums = [None] * len(OFFSETS)
        for b in range(NB):
            both = jnp.dot(oh[b, here, :], t2[...], preferred_element_type=F32)
            picked = both[:, :width] + both[:, width:]
            for n in range(len(OFFSETS)):
                term = wd[b, n, here, :] * picked
                sums[n] = term if sums[n] is None else sums[n] + term
        total = sums[OFFSETS.index(0)]
        for n, d in enumerate(OFFSETS):
            if d:
                total = total + pltpu.roll(sums[n], -d % width, 1)
        warp[pl.ds(YR + c * width, width), :] = total
        apart = total - img_v[0, here, :]
        for n, d in enumerate(OFFSETS):
            mis[n, here, :] = pltpu.roll(apart, d % width, 1) if d else apart
        if (c + 1) * width == YR:
            pl.when(me_k > 0)(warp_halo[0].start)
    pl.when(me_k < slabs - 1)(warp_halo[1].start)

    block = 16
    for c in range(rows // width):
        for q in range(width // block):
            here = pl.ds(c * width + q * block, block)
            apart = [mis[n, here, :] for n in range(len(OFFSETS))]
            for b in range(NB):
                total = wd[b, 0, here, :] * apart[0]
                for n in range(1, len(OFFSETS)):
                    total = total + wd[b, n, here, :] * apart[n]
                hi, lo = halves(total)
                there = pl.ds((c * NB + b) * width + q * block, block)
                place[there, :width] = hi
                place[there, width:] = lo

    sent(first)
    second = peers("slab", to_slab, lambda i: retbox.at[own, :], b_send, b_recv)
    for part_of in range(2):
        here = pl.ds(part_of * (slots // 2), slots // 2)
        both = jnp.dot(oht[here, :], place[...], preferred_element_type=F32)
        outbox[here, :] = both[:, :width] + both[:, width:]
        for copy, to in zip(second, rest["slab"]):
            pl.when((to >= slabs // 2) == bool(part_of))(copy.start)
    retbox[own, :] = outbox[own, :]

    @pl.when(linked)
    def _():
        stif_far.wait_recv()
        start(shared)

    ost[...] = jnp.transpose(os[...].astype(F32)).astype(BF)

    halo_got(warp_halo)
    loads[7].wait()
    lane_p = lax.broadcasted_iota(jnp.int32, (YR, width), 1)
    row_p = lax.broadcasted_iota(jnp.int32, (YR, width), 0)

    def shifted(x):
        left = jnp.where(lane_p == 0, 0.0, pltpu.roll(x, 1, 1))
        right = jnp.where(lane_p == width - 1, 0.0, pltpu.roll(x, width - 1, 1))
        above = jnp.where(row_p == 0, 0.0, pltpu.roll(x, 1, 0))
        below = jnp.where(row_p == YR - 1, 0.0, pltpu.roll(x, YR - 1, 0))
        return left, right, above, below

    def along(x, dim):
        left, right, above, below = shifted(x)
        return right - left if dim else below - above

    for a in range(3):

        @pl.loop(0, rows // YR)
        def _(p):
            plane = lambda i: pl.ds(pl.multiple_of((p + i) * YR, YR), YR)
            if a == 2:
                slope = warp[plane(2), :] - warp[plane(0), :]
            else:
                slope = along(warp[plane(1), :], 1 - a)
            field[a, plane(2), :] = vel_v[0, a, plane(0), :] - (0.5 * FORCE) * mis[2, plane(0), :] * slope

        halo_start(field_halo[a])

    stif_near.wait_recv()

    @pl.when(linked)
    def _():
        got(shared)

    @pl.loop(0, rows // YR + 2)
    def _(p):
        plane = me_k * (rows // YR) + p
        inside = jnp.where(jnp.logical_and(plane >= 1, plane <= slabs * (rows // YR)), 1.0, 0.0)
        here = pl.ds(pl.multiple_of(p * YR, YR), YR)
        centre = stif[pl.ds(pl.multiple_of((p + 1) * YR, YR), YR), :]
        before = stif[here, :]
        after = stif[pl.ds(pl.multiple_of((p + 2) * YR, YR), YR), :]
        near = shifted(centre)
        scale = inside * HALF_DT
        edges = (lane_p == 0, lane_p == width - 1, row_p == 0, row_p == YR - 1)
        spent = 6.0 * centre + before + after
        for n in range(4):
            coef[n, here, :] = jnp.where(edges[n], 0.0, scale * (centre + near[n]))
            spent = spent + near[n]
        coef[4, here, :] = scale * (centre + before)
        coef[5, here, :] = scale * (centre + after)
        coef[6, here, :] = inside - scale * spent

    got(second)
    hi, lo = halves(retbox[...])
    back = jnp.concatenate([hi, lo], axis=1)
    third = peers(
        "subj", lambda s: rowg.at[pl.ds(pl.multiple_of(s * part, part), part), :], lambda i: subbox.at[i], c_send, c_recv,
    )
    for part_of in range(2):
        here = pl.ds(part_of * (rows // 2), rows // 2)
        both = jnp.dot(ost[here, :], back, preferred_element_type=F32)
        rowg[here, :] = both[:, :width] + both[:, width:]
        for copy, to in zip(third, rest["subj"]):
            pl.when((to >= subjects // 2) == bool(part_of))(copy.start)
    total = rowg[mine, :]
    got(third)
    for i in range(subjects - 1):
        total = total + subbox[i]
    tout[mine, :] = tmpl_v[mine, :] - (RATE / subjects) * total
    fourth = peers("subj", lambda s: tout.at[mine, :], lambda i: tout.at[mine, :], d_send, d_recv)
    start(fourth)

    def step(src, lead, p, q):
        at = lambda i: pl.ds(pl.multiple_of(i * YR, YR), YR)
        x = src[lead, at(p), :]
        c = lambda n: coef[n, at(q), :]
        out = c(6) * x
        out = out + c(0) * pltpu.roll(x, 1, 1)
        out = out + c(1) * pltpu.roll(x, width - 1, 1)
        out = out + c(2) * pltpu.roll(x, 1, 0)
        out = out + c(3) * pltpu.roll(x, YR - 1, 0)
        out = out + c(4) * src[lead, at(p - 1), :]
        return out + c(5) * src[lead, at(p + 1), :]

    def diffuse(a):
        halo_got(field_halo[a])

        @pl.loop(0, rows // YR + 2)
        def _(p):
            field1[a, pl.ds(pl.multiple_of(p * YR, YR), YR), :] = step(field, a, p + 1, p)

        @pl.loop(0, rows // YR)
        def _(p):
            vout[0, a, pl.ds(pl.multiple_of(p * YR, YR), YR), :] = step(field1, a, p + 1, p + 1)

    for a in range(3):
        diffuse(a)

    for group in (second, third):
        sent(group)
    for h in (warp_halo, *field_halo):
        halo_sent(h)
    stif_near.wait_send()

    @pl.when(linked)
    def _():
        stif_far.wait_send()
        sent(shared)

    got(fourth)
    sent(fourth)


def store(template, velocity, tout, vout, sem):
    one = pltpu.make_async_copy(velocity, vout, sem.at[0])
    two = pltpu.make_async_copy(template, tout, sem.at[1])
    one.start()
    two.start()
    one.wait()
    two.wait()


def per_device(subjects, slabs, template, images, velocity, stiffness, send_rows, ref_slot, columns, weights):
    rows, width = template.shape
    cap = send_rows.shape[3]
    slots = slabs * cap
    planes = rows // YR
    hbm_space = pl.BlockSpec(memory_space=pltpu.HBM)
    dma = pltpu.SemaphoreType.DMA
    vm = pltpu.VMEM
    scratch = [
        vm((rows, width), F32),
        vm((1, rows, width), F32),
        vm((1, 3, rows, width), F32),
        vm((1, 1, slabs, cap), jnp.int32),
        vm((1, NB, rows), jnp.int32),
        vm((rows * NB, width), jnp.int32),
        vm((rows * NB, width), BF),
        vm((rows * NB, width), F32),
        vm((NB, len(OFFSETS), rows, width), F32),
        vm((NB, rows, slots), BF),
        vm((slots, NB * rows), BF),
        vm((slots, rows), BF),
        vm((rows, slots), BF),
        vm((slots, width), F32),
        vm((slots, width), F32),
        vm((slots, 2 * width), BF),
        vm((rows + 2 * YR, width), F32),
        vm((len(OFFSETS), rows, width), F32),
        vm((NB * rows, 2 * width), BF),
        vm((slots, width), F32),
        vm((rows, width), F32),
        vm((subjects - 1, rows // subjects, width), F32),
        vm((7, rows + 2 * YR, width), F32),
        vm((rows + 4 * YR, width), F32),
        vm((3, rows + 4 * YR, width), F32),
        vm((3, rows + 2 * YR, width), F32),
        dma((8,)),
        dma((slabs,)), dma((slabs,)), dma((slabs,)), dma((slabs,)),
        dma((subjects,)), dma((subjects,)), dma((subjects,)), dma((subjects,)),
        dma((subjects,)), dma((subjects,)), dma((10,)), dma((10,)),
    ]
    outs = (
        jax.ShapeDtypeStruct((rows, width), F32),
        jax.ShapeDtypeStruct((1, 3, rows, width), F32),
    )
    vmem_space = pl.BlockSpec(memory_space=vm)
    new = pl.pallas_call(
        functools.partial(kernel, subjects, slabs, cap),
        out_shape=tuple(vm(o.shape, o.dtype) for o in outs),
        in_specs=[hbm_space] * 8,
        out_specs=(vmem_space, vmem_space),
        scratch_shapes=scratch,
        compiler_params=pltpu.CompilerParams(
            collective_id=0, has_side_effects=True, vmem_limit_bytes=62 * 2**20
        ),
    )(
        template, images, velocity, stiffness, send_rows,
        jnp.transpose(ref_slot, (0, 2, 1)),
        columns.reshape(rows * NB, width),
        weights.reshape(rows * NB, width),
    )
    return pl.pallas_call(
        store,
        out_shape=outs,
        in_specs=[pl.BlockSpec(memory_space=pl.ANY)] * 2,
        out_specs=(hbm_space, hbm_space),
        scratch_shapes=[dma((2,))],
        compiler_params=pltpu.CompilerParams(vmem_limit_bytes=2**20),
    )(*new)


def solution(mesh):
    return jax.shard_map(
        functools.partial(per_device, mesh.shape["subj"], mesh.shape["slab"]),
        mesh=mesh,
        in_specs=(
            P("slab", None),
            P("subj", "slab", None),
            P("subj", None, "slab", None),
            P("slab", None),
            P("subj", "slab", None, None),
            P("subj", "slab", None),
            P("subj", "slab", None, None),
            P("subj", "slab", None, None),
        ),
        out_specs=(P("slab", None), P("subj", None, "slab", None)),
        check_vma=False,
    )
```
